128 devices in a mesh: dp: 8 (over y_lo, z), tp: 16 (over y_hi, x, core).
Axes of the slice: x: 4, y: 4 (y_hi: 2, y_lo: 2; y = y_hi * 2 + y_lo), z: 4, core: 2. Of those that a mesh axis runs over, the one named last changes fastest.
Arguments:
- tokens: bfloat16 [4096, 2304], P(('dp', 'tp')), may hold values from -36 to 36
- gain_pre: float32 [2304], replicated, may hold values from 0.1 to 1.9
- gain_post: float32 [2304], replicated, may hold values from 0.1 to 1.9
- gate_weight: bfloat16 [2304, 18432], P(None, 'tp'), may hold values from -0.125 to 0.125
- up_weight: bfloat16 [2304, 18432], P(None, 'tp'), may hold values from -0.125 to 0.125
- down_weight: bfloat16 [18432, 2304], P('tp'), may hold values from -0.046875 to 0.046875
- cotangent: bfloat16 [4096, 2304], P(('dp', 'tp')), may hold values from -1.5 to 1.5
Outputs:
- block_out: bfloat16 [4096, 2304], P(('dp', 'tp'))
- tokens_grad: bfloat16 [4096, 2304], P(('dp', 'tp'))
- gain_pre_grad: float32 [2304], replicated
- gain_post_grad: float32 [2304], replicated
- gate_grad: float32 [2304, 18432], P('dp', 'tp')
- up_grad: float32 [2304, 18432], P('dp', 'tp')
- down_grad: float32 [18432, 2304], P(('tp', 'dp'))
The draws below stay inside these ranges and needn't reach their ends.
All inputs are finite; a program needn't handle non-finite values.
Results may differ from the reference program's by a relative error of at most 0.02.
Values may be sent and summed in bfloat16 or wider, within the bound.
A program may use at most 128 MiB of HBM per device.

```python
import math
import jax
import jax.numpy as jnp
from jax import lax

D = 2304
FF = 18432
ROWS = 512
TOKENS = 4096
N_DP = 8


def draw_tokens(key, part):
    key = jax.random.fold_in(key, 11)
    key_main, key_rows, key_cols = jax.random.split(key, 3)
    row_scale = jnp.exp(jax.random.uniform(key_rows, (TOKENS, 1), jnp.float32, math.log(0.5), math.log(5.0)))
    col_scale = jnp.exp(jax.random.uniform(key_cols, (1, D), jnp.float32, math.log(0.6), math.log(1.8)))
    base_values = jnp.clip(jax.random.normal(key_main, (TOKENS, D), jnp.float32), -4.0, 4.0)
    return (base_values * row_scale * col_scale).astype(jnp.bfloat16)


def draw_cotangent(key, part):
    key = jax.random.fold_in(key, 23)
    position = jnp.arange(TOKENS, dtype=jnp.float32)[:, None] / TOKENS
    base_values = jnp.clip(jax.random.normal(key, (TOKENS, D), jnp.float32), -4.0, 4.0)
    ramp_scale = 0.5 + position
    return (0.25 * base_values * ramp_scale).astype(jnp.bfloat16)


def block_scale(stream_key, extent, pieces, smallest, largest):
    level = 1.0
    for axis_at, parts in pieces:
        heights = jax.random.uniform(jax.random.fold_in(jax.random.fold_in(stream_key, 6), axis_at), (parts,), jnp.float32, smallest / len(pieces), largest / len(pieces))
        level = level * jnp.repeat(jnp.exp(heights), extent[axis_at] // parts).reshape((-1,) + (1,) * (len(extent) - 1 - axis_at))
    return level


def scatter_about(key, shape, deviation, most, cuts=(), kind=jnp.bfloat16):
    values = jax.random.normal(key, shape, jnp.float32) * deviation
    if len(cuts) > 0:
        values = block_scale(key, shape, cuts, -0.22, 0.18) * values
    return jnp.clip(values, min=-most, max=most).astype(kind)


def setup_inputs(seed: int = 0) -> dict:
    seeds = jax.random.split(jax.random.key(seed), 8)
    return {
        "tokens": draw_tokens(jax.random.fold_in(seeds[7], 71), 0),
        "gain_pre": jnp.clip(1.0 + 0.18 * jax.random.normal(seeds[1], (D,), jnp.float32), 0.1, 1.9),
        "gain_post": jnp.clip(1.0 + 0.18 * jax.random.normal(seeds[2], (D,), jnp.float32), 0.1, 1.9),
        "gate_weight": scatter_about(seeds[3], (D, FF), D ** -0.5, 0.125, ((1, 16),)),
        "up_weight": scatter_about(seeds[4], (D, FF), D ** -0.5, 0.125, ((1, 16),)),
        "down_weight": scatter_about(seeds[5], (FF, D), FF ** -0.5, 0.046875, ((0, 16),)),
        "cotangent": draw_cotangent(jax.random.fold_in(seeds[7], 71), 0),
    }


epsilon = 1e-06
root_two_pi = 0.7978845608028654

def gelu_pair(values):
    tanh_arg = root_two_pi * (values + 0.044715 * values * values * values)
    hyper = jnp.tanh(tanh_arg)
    gelu_value = 0.5 * values * (1.0 + hyper)
    gelu_slope = 0.5 * (1.0 + hyper) + 0.5 * values * (1.0 - hyper * hyper) * root_two_pi * (1.0 + 3.0 * 0.044715 * values * values)
    return (gelu_value, gelu_slope)

def norm_parts(values):
    recip = lax.rsqrt(lax.optimization_barrier(jnp.mean(values * values, axis=-1, keepdims=True)) + epsilon)
    return (values * recip, recip)

def norm_back(grad_in, scaled, recip, gain):
    weighted = grad_in * gain
    return recip * (weighted - scaled * lax.optimization_barrier(jnp.mean(weighted * scaled, axis=-1, keepdims=True)))

def reference(tokens, gain_pre, gain_post, gate_weight, up_weight, down_weight, cotangent):
    group_tokens = tokens.reshape(N_DP, ROWS, D)
    group_cot = cotangent.reshape(N_DP, ROWS, D)

    def per_group(running, inputs):
        token_rows, cot_rows = inputs
        inputs_f = token_rows.astype(jnp.float32)
        scaled_in, recip_in = norm_parts(inputs_f)
        normed = (scaled_in * gain_pre).astype(jnp.bfloat16)
        gate_pre = jnp.dot(normed, gate_weight, preferred_element_type=jnp.float32)
        up_pre = jnp.dot(normed, up_weight, preferred_element_type=jnp.float32)
        activated, gelu_slope = gelu_pair(gate_pre)
        hidden = (activated * up_pre).astype(jnp.bfloat16)
        mixed = jnp.dot(hidden, down_weight, preferred_element_type=jnp.float32)
        scaled_mix, recip_mix = norm_parts(mixed)
        block_out = (inputs_f + scaled_mix * gain_post).astype(jnp.bfloat16)
        cot_f = cot_rows.astype(jnp.float32)
        post_term = lax.optimization_barrier(jnp.sum(cot_f * scaled_mix, axis=0))
        mix_grad = norm_back(cot_f, scaled_mix, recip_mix, gain_post).astype(jnp.bfloat16)
        hidden_grad = lax.dot_general(mix_grad, down_weight, (((1,), (1,)), ((), ())), preferred_element_type=jnp.float32)
        down_term = lax.dot_general(hidden, mix_grad, (((0,), (0,)), ((), ())), preferred_element_type=jnp.float32).astype(jnp.bfloat16)
        up_pre_grad = (hidden_grad * activated).astype(jnp.bfloat16)
        gate_pre_grad = (hidden_grad * up_pre * gelu_slope).astype(jnp.bfloat16)
        gate_term = lax.dot_general(normed, gate_pre_grad, (((0,), (0,)), ((), ())), preferred_element_type=jnp.float32).astype(jnp.bfloat16)
        up_term = lax.dot_general(normed, up_pre_grad, (((0,), (0,)), ((), ())), preferred_element_type=jnp.float32).astype(jnp.bfloat16)
        normed_grad = lax.dot_general(gate_pre_grad, gate_weight, (((1,), (1,)), ((), ())), preferred_element_type=jnp.float32)
        normed_grad = normed_grad + lax.dot_general(up_pre_grad, up_weight, (((1,), (1,)), ((), ())), preferred_element_type=jnp.float32)
        pre_term = lax.optimization_barrier(jnp.sum(normed_grad * scaled_in, axis=0))
        tokens_grad = (cot_f + norm_back(normed_grad, scaled_in, recip_in, gain_pre)).astype(jnp.bfloat16)
        gate_sum, up_sum, down_sum, pre_sum, post_sum = running
        running = (gate_sum + gate_term.astype(jnp.float32), up_sum + up_term.astype(jnp.float32), down_sum + down_term.astype(jnp.float32), pre_sum + pre_term, post_sum + post_term)
        return (running, (block_out, tokens_grad))
    start_carry = (jnp.zeros((D, FF), jnp.float32), jnp.zeros((D, FF), jnp.float32), jnp.zeros((FF, D), jnp.float32), jnp.zeros((D,), jnp.float32), jnp.zeros((D,), jnp.float32))
    running, outputs = lax.scan(per_group, start_carry, (group_tokens, group_cot))
    gate_grad, up_grad, down_grad, gain_pre_grad, gain_post_grad = running
    block_out = outputs[0].reshape(TOKENS, D)
    tokens_grad = outputs[1].reshape(TOKENS, D)
    return (block_out, tokens_grad, gain_pre_grad, gain_post_grad, gate_grad, up_grad, down_grad)
```

```python
import jax
import jax.numpy as jnp
from jax import lax
from jax.experimental import pallas as pl
from jax.experimental.pallas import tpu as pltpu
from jax.sharding import PartitionSpec as P

epsilon = 1e-06
root_two_pi = 0.7978845608028654
MESH = pl.DeviceIdType.MESH
D = 2304
F = 1152
B = 32
T = 384
f32 = jnp.float32
bf16 = jnp.bfloat16


def gelu_pair(values):
    tanh_arg = root_two_pi * (values + 0.044715 * values * values * values)
    hyper = jnp.tanh(tanh_arg)
    gelu_value = 0.5 * values * (1.0 + hyper)
    gelu_slope = 0.5 * (1.0 + hyper) + 0.5 * values * (1.0 - hyper * hyper) * root_two_pi * (
        1.0 + 3.0 * 0.044715 * values * values
    )
    return (gelu_value, gelu_slope)


def nt(a, b):
    return lax.dot_general(a, b, (((1,), (1,)), ((), ())), preferred_element_type=f32)


def nn(a, b):
    return jnp.dot(a, b, preferred_element_type=f32)


def tile(j, width=T):
    return pl.ds(pl.multiple_of(j * width, 128), width)


def kernel(
    tok, cot, gpre, gpost, wg_h, wu_h, wd_h,
    bout, tgrad, gain_pre_out, gain_post_out, d_own, d_a, d_b, g_own, g_a, g_b, u_own, u_a, u_b,
    wg, wu, wd, nbuf, mgbuf, act, us, hown, ht, ntr, part, crecv, xrecv, ysend, yrecv,
    zd, zg, zu, zdf, zgf, zuf, gv, gc, gx, gy, gz,
    wsem, ag1s, ag1r, ag2s, ag2r, rs1s, rs1r, rs2s, rs2r, zs, zr, zl, gs, gr,
):
    dp, tp = lax.axis_index("dp"), lax.axis_index("tp")
    c = tp % 2
    x = (tp // 2) % 4
    yh = tp // 8
    yl = dp // 4
    z = dp % 4
    y = yh * 2 + yl

    def dev(dx=0, dy=0, dz=0, dc=0):
        yy = (y + dy) % 4
        return ((yy % 2) * 4 + (z + dz) % 4, ((yy // 2) * 4 + (x + dx) % 4) * 2 + (c + dc) % 2)

    loads = [
        pltpu.make_async_copy(h, v, wsem.at[i])
        for i, (h, v) in enumerate(((wg_h, wg), (wu_h, wu), (wd_h, wd)))
    ]
    for load in loads:
        load.start()

    barrier = pltpu.get_barrier_semaphore()
    offs = [dict(dc=1)] + [{a: k} for a in ("dx", "dy", "dz") for k in (1, 2, 3)]
    for o in offs:
        pl.semaphore_signal(barrier, inc=1, device_id=dev(**o), device_id_type=MESH)

    def remote(src, dst, s, r, to):
        return pltpu.make_async_remote_copy(
            src_ref=src, dst_ref=dst, send_sem=s, recv_sem=r, device_id=to, device_id_type=MESH
        )

    def blk(buf, df, ds, core=None):
        dx = df * (1 - c) + ds * c
        dy = df * c + ds * (1 - c)
        xx, yy = (x + dx) % 4, (y + dy) % 4
        return buf.at[yy % 2, yy // 2, xx, c]

    def other_blk(buf, df, ds):
        dx = df * c + ds * (1 - c)
        dy = df * (1 - c) + ds * c
        xx, yy = (x + dx) % 4, (y + dy) % 4
        return buf.at[yy % 2, yy // 2, xx, 1 - c]

    def to_f(sign):
        return dev(dx=(1 - c) * (sign % 4), dy=c * (sign % 4))

    def to_s(sign):
        return dev(dx=c * (sign % 4), dy=(1 - c) * (sign % 4))

    def gather(buf, ss, rr):
        sent = []

        def send(i, ref, to):
            cp = remote(ref, ref, ss.at[i], rr.at[i], to)
            cp.start()
            sent.append(cp)

        def got(i, ref):
            remote(ref, ref, ss.at[i], rr.at[i], dev(dc=1)).wait_recv()

        def core(df, ds):
            send(16 + ds * 4 + df, blk(buf, df, ds), dev(dc=1))

        own = blk(buf, 0, 0)
        send(0, own, to_f(1))
        send(1, own, to_f(-1))
        send(4, own, to_s(1))
        send(8, own, to_s(-1))
        core(0, 0)
        got(0, blk(buf, 3, 0))
        send(2, blk(buf, 3, 0).at[pl.ds(0, 16)], to_f(1))
        send(7, blk(buf, 3, 0), to_s(1))
        send(11, blk(buf, 3, 0), to_s(-1))
        core(3, 0)
        got(1, blk(buf, 1, 0))
        send(3, blk(buf, 1, 0).at[pl.ds(16, 16)], to_f(-1))
        send(5, blk(buf, 1, 0), to_s(1))
        send(9, blk(buf, 1, 0), to_s(-1))
        core(1, 0)
        got(2, blk(buf, 2, 0).at[pl.ds(0, 16)])
        got(3, blk(buf, 2, 0).at[pl.ds(16, 16)])
        send(6, blk(buf, 2, 0), to_s(1))
        send(10, blk(buf, 2, 0), to_s(-1))
        core(2, 0)
        for df, fwd_a, fwd_b in ((0, 12, None), (1, 13, None), (3, None, 14), (2, None, 15)):
            got(4 + df, blk(buf, df, 3))
            if fwd_a is not None:
                send(fwd_a, blk(buf, df, 3), to_s(1))
            core(df, 3)
            got(8 + df, blk(buf, df, 1))
            if fwd_b is not None:
                send(fwd_b, blk(buf, df, 1), to_s(-1))
            core(df, 1)
        for i, df in ((12, 0), (13, 1), (14, 3), (15, 2)):
            got(i, blk(buf, df, 2))
            core(df, 2)
        for ds in range(4):
            for df in range(4):
                got(16 + ds * 4 + df, other_blk(buf, df, ds))
        return sent

    def core_send(half, i, ss, rr):
        cp = remote(part.at[half, :, 1 - c], crecv.at[i], ss.at[i], rr.at[i], dev(dc=1))
        cp.start()
        return cp

    def core_add(half, i, ss, rr):
        remote(crecv.at[i], crecv.at[i], ss.at[i], rr.at[i], dev(dc=1)).wait_recv()

        def one(k, _):
            part[half, k, c] = (part[half, k, c].astype(f32) + crecv[i, k].astype(f32)).astype(bf16)
            return 0

        lax.fori_loop(0, 4, one, 0)

    def x_send(half, i, ss, rr):
        out = []
        for dx in (2, 1, 3):
            k = 2 + i * 3 + dx - 1
            cp = remote(
                part.at[half, (x + dx) % 4, c], xrecv.at[i, dx - 1], ss.at[k], rr.at[k], dev(dx=dx)
            )
            cp.start()
            out.append(cp)
        return out

    def x_sum(half, i, ss, rr):
        for dx in (1, 3, 2):
            k = 2 + i * 3 + dx - 1
            ref = xrecv.at[i, dx - 1]
            remote(ref, ref, ss.at[k], rr.at[k], dev(dx=dx)).wait_recv()
        total = part[half, x, c].astype(f32)
        for dx in (1, 3, 2):
            total = total + xrecv[i, dx - 1].astype(f32)
        return total

    def y_send(total, ss, rr):
        ysend[...] = total.astype(bf16)
        cp = remote(ysend, yrecv, ss.at[8], rr.at[8], dev(dy=2))
        cp.start()
        return cp

    def y_sum(total, ss, rr):
        remote(yrecv, yrecv, ss.at[8], rr.at[8], dev(dy=2)).wait_recv()
        return total + yrecv[...].astype(f32)

    tok_f = tok[...].astype(f32)
    recip_in = lax.rsqrt(jnp.mean(tok_f * tok_f, axis=-1, keepdims=True) + epsilon)
    nbuf[yl, yh, x, c] = (tok_f * recip_in * gpre[...]).astype(bf16)

    pl.semaphore_wait(barrier, len(offs))
    sent1 = gather(nbuf, ag1s, ag1r)
    for load in loads:
        load.wait()

    def forward(yy, is_own):
        a, b = yy % 2, yy // 2
        k = a * 2 + b

        def one(j, _):
            rows = nbuf[a, b].reshape(256, D)
            gate = nn(rows, wg[:, tile(j)])
            up = nn(rows, wu[:, tile(j)])
            value, slope = gelu_pair(gate)
            hidden = (value * up).astype(bf16)
            act[a, b, :, tile(j)] = value.astype(bf16)
            us[a, b, :, tile(j)] = (up * slope).astype(bf16)
            if is_own:
                hown[b, :, tile(j)] = hidden
            ht[tile(j), tile(k, 256)] = hidden.T
            return 0

        lax.fori_loop(0, 3, one, 0)

    def down(half):
        def one(j, _):
            part[half, :, :, :, tile(j)] = (
                nn(hown[half], wd[:, tile(j)]).astype(bf16).reshape(4, 2, B, T)
            )
            return 0

        lax.fori_loop(0, 6, one, 0)

    forward((y + 2) % 4, True)
    down(1 - yh)
    pend = [core_send(1 - yh, 0, rs1s, rs1r)]
    forward(y, True)
    core_add(1 - yh, 0, rs1s, rs1r)
    pend += x_send(1 - yh, 0, rs1s, rs1r)
    down(yh)
    pend.append(core_send(yh, 1, rs1s, rs1r))
    core_add(yh, 1, rs1s, rs1r)
    pend += x_send(yh, 1, rs1s, rs1r)
    forward((y + 1) % 4, False)
    pend.append(y_send(x_sum(1 - yh, 0, rs1s, rs1r), rs1s, rs1r))
    forward((y + 3) % 4, False)
    mixed = y_sum(x_sum(yh, 1, rs1s, rs1r), rs1s, rs1r)

    recip_mix = lax.rsqrt(jnp.mean(mixed * mixed, axis=-1, keepdims=True) + epsilon)
    scaled_mix = mixed * recip_mix
    cot_f = cot[...].astype(f32)
    weighted = cot_f * gpost[...]
    mix_grad = recip_mix * (
        weighted - scaled_mix * jnp.mean(weighted * scaled_mix, axis=-1, keepdims=True)
    )
    mgbuf[yl, yh, x, c] = mix_grad.astype(bf16)
    bout[...] = (tok[...].astype(f32) + scaled_mix * gpost[...]).astype(bf16)
    gv[...] = jnp.zeros_like(gv)
    gv[1:2, :] = jnp.sum(cot_f * scaled_mix, axis=0, keepdims=True)
    for cp in pend + sent1:
        cp.wait_send()

    sent2 = gather(mgbuf, ag2s, ag2r)

    def turn(k, _):
        rows = nbuf[k // 2, k % 2].reshape(256, D)
        del rows

        def one(j, _):
            cols = pl.ds(pl.multiple_of(yl * F + j * T, 128), T)
            ntr[tile(j), tile(k, 256)] = nbuf[k // 2, k % 2, :, :, :, cols].reshape(256, T).T
            return 0

        lax.fori_loop(0, 3, one, 0)
        return 0

    lax.fori_loop(0, 4, turn, 0)

    units = {}
    sent3 = []

    def halves(ref, kind, k):
        if kind == "d":
            return ref.at[:, pl.ds(k * T, T)]
        return ref.at[pl.ds(k * 144, 144)]

    bufs = {"d": (zd, zdf, d_own, d_a, d_b, 0), "g": (zg, zgf, g_own, g_a, g_b, 3), "u": (zu, zuf, u_own, u_a, u_b, 6)}

    def z_first(kind, j):
        buf, fwd, own, _, _, base = bufs[kind]
        q = (base + j) * 4
        for k, dz in ((0, 1), (1, 3)):
            cp = remote(
                halves(buf.at[j, (z + 2) % 4], kind, k), fwd.at[j, k], zs.at[q + k], zr.at[q + k], dev(dz=dz)
            )
            cp.start()
            sent3.append(cp)
        width = 2 * T if kind == "d" else T
        cp = pltpu.make_async_copy(buf.at[j, z], own.at[:, pl.ds(j * width, width)], zl.at[base + j])
        cp.start()
        units[kind, j] = cp

    def z_second(kind, j):
        buf, fwd, _, out_a, out_b, base = bufs[kind]
        q = (base + j) * 4
        width = 2 * T if kind == "d" else T
        for k, dz, out in ((0, 1, out_a), (1, 3, out_b)):
            ref = fwd.at[j, k]
            remote(ref, ref, zs.at[q + k], zr.at[q + k], dev(dz=dz)).wait_recv()
            to = (z + dz) % 4
            if kind == "d":
                cols = pl.ds(k * T, T)
                buf[j, to, :, cols] = (buf[j, to, :, cols].astype(f32) + fwd[j, k].astype(f32)).astype(bf16)
            else:
                rows = pl.ds(k * 144, 144)
                buf[j, to, rows] = (buf[j, to, rows].astype(f32) + fwd[j, k].astype(f32)).astype(bf16)
            cp = remote(
                buf.at[j, to], out.at[:, pl.ds(j * width, width)], zs.at[q + 2 + k], zr.at[q + 2 + k], dev(dz=dz)
            )
            cp.start()
            sent3.append(cp)

    def down_grad(j):
        def one(i, _):
            lhs = ht[pl.ds(pl.multiple_of(yl * 576, 64), 576), :]
            cols = pl.ds(pl.multiple_of((j * 2 + i) * T, 128), T)
            rhs = mgbuf[:, :, :, :, :, cols].reshape(1024, T)
            zd[j, :, :, tile(i)] = nn(lhs, rhs).astype(bf16).reshape(4, 144, T)
            return 0

        lax.fori_loop(0, 2, one, 0)

    def hidden_grad(j):
        def one(k, _):
            a, b = k // 2, k % 2
            grad = nt(mgbuf[a, b].reshape(256, D), wd[pl.ds(j * T, T), :])
            cols = pl.ds(j * T, T)
            act[a, b, :, cols] = (grad * act[a, b, :, cols].astype(f32)).astype(bf16)
            us[a, b, :, cols] = (grad * us[a, b, :, cols].astype(f32)).astype(bf16)
            return 0

        lax.fori_loop(0, 4, one, 0)

    def in_grad(buf, src, j):
        def one(i, _):
            rhs = src[:, :, :, pl.ds(j * T, T)].reshape(1024, T)
            lhs = ntr[pl.ds(pl.multiple_of(i * 288, 32), 288), :]
            buf[j, i] = nn(lhs, rhs).astype(bf16)
            return 0

        lax.fori_loop(0, 4, one, 0)

    for j in range(3):
        down_grad(j)
        z_first("d", j)
    for j in range(3):
        hidden_grad(j)
        in_grad(zg, us, j)
        z_first("g", j)
        z_second("d", j)
        in_grad(zu, act, j)
        z_first("u", j)
        if j >= 1:
            z_second("g", j - 1)
            z_second("u", j - 1)

    def normed_grad(half):
        def one(j, _):
            total = nt(us[yl, half], wg[tile(j), :]) + nt(act[yl, half], wu[tile(j), :])
            part[half, :, :, :, tile(j)] = total.astype(bf16).reshape(4, 2, B, T)
            return 0

        lax.fori_loop(0, 6, one, 0)

    normed_grad(1 - yh)
    pend = [core_send(1 - yh, 0, rs2s, rs2r)]
    z_second("g", 2)
    z_second("u", 2)
    normed_grad(yh)
    pend.append(core_send(yh, 1, rs2s, rs2r))
    core_add(1 - yh, 0, rs2s, rs2r)
    pend += x_send(1 - yh, 0, rs2s, rs2r)
    core_add(yh, 1, rs2s, rs2r)
    pend += x_send(yh, 1, rs2s, rs2r)
    pend.append(y_send(x_sum(1 - yh, 0, rs2s, rs2r), rs2s, rs2r))
    grad_in = y_sum(x_sum(yh, 1, rs2s, rs2r), rs2s, rs2r)
    tok_f = tok[...].astype(f32)
    recip_in = lax.rsqrt(jnp.mean(tok_f * tok_f, axis=-1, keepdims=True) + epsilon)
    scaled_in = tok_f * recip_in
    weighted = grad_in * gpre[...]
    back = recip_in * (weighted - scaled_in * jnp.mean(weighted * scaled_in, axis=-1, keepdims=True))
    tgrad[...] = (cot[...].astype(f32) + back).astype(bf16)
    gv[0:1, :] = jnp.sum(grad_in * scaled_in, axis=0, keepdims=True)

    cp = remote(gv, gc, gs.at[0], gr.at[0], dev(dc=1))
    cp.start()
    cp.wait()
    value = gv[...] + gc[...]
    for n, (slots, axis, at) in enumerate(((gx, "dx", x), (gy, "dy", y), (gz, "dz", z))):
        slots[at] = value
        cps = []
        for k in (1, 2, 3):
            i = 1 + n * 3 + k - 1
            cp = remote(slots.at[at], slots.at[at], gs.at[i], gr.at[i], dev(**{axis: k}))
            cp.start()
            cps.append(cp)
        for k in (1, 2, 3):
            i = 1 + n * 3 + k - 1
            ref = slots.at[(at + 4 - k) % 4]
            remote(ref, ref, gs.at[i], gr.at[i], dev(**{axis: k})).wait_recv()
        for cp in cps:
            cp.wait_send()
        value = (slots[0] + slots[1]) + (slots[2] + slots[3])
    gain_pre_out[...] = value[0:1, :]
    gain_post_out[...] = value[1:2, :]

    for kind in "dgu":
        _, _, own, out_a, out_b, base = bufs[kind]
        width = 2 * T if kind == "d" else T
        for j in range(3):
            q = (base + j) * 4
            for k, out in ((0, out_a), (1, out_b)):
                ref = out.at[:, pl.ds(j * width, width)]
                remote(ref, ref, zs.at[q + 2 + k], zr.at[q + 2 + k], dev(dz=1)).wait_recv()
            units[kind, j].wait()
    for cp in pend + sent2 + sent3:
        cp.wait_send()


def local(tokens, gain_pre, gain_post, gate_weight, up_weight, down_weight, cotangent):
    vm = pl.BlockSpec(memory_space=pltpu.VMEM)
    hbm = pl.BlockSpec(memory_space=pl.ANY)
    S = jax.ShapeDtypeStruct
    dma = pltpu.SemaphoreType.DMA
    outs = pl.pallas_call(
        kernel,
        out_shape=(
            [S((B, D), bf16), S((B, D), bf16), S((1, D), f32), S((1, D), f32)]
            + [S((144, D), bf16)] * 3
            + [S((288, F), bf16)] * 6
        ),
        in_specs=[vm] * 4 + [hbm] * 3,
        out_specs=[vm] * 4 + [hbm] * 9,
        scratch_shapes=[
            pltpu.VMEM((D, F), bf16),
            pltpu.VMEM((D, F), bf16),
            pltpu.VMEM((F, D), bf16),
            pltpu.VMEM((2, 2, 4, 2, B, D), bf16),
            pltpu.VMEM((2, 2, 4, 2, B, D), bf16),
            pltpu.VMEM((2, 2, 256, F), bf16),
            pltpu.VMEM((2, 2, 256, F), bf16),
            pltpu.VMEM((2, 256, F), bf16),
            pltpu.VMEM((F, 1024), bf16),
            pltpu.VMEM((F, 1024), bf16),
            pltpu.VMEM((2, 4, 2, B, D), bf16),
            pltpu.VMEM((2, 4, B, D), bf16),
            pltpu.VMEM((2, 3, B, D), bf16),
            pltpu.VMEM((B, D), bf16),
            pltpu.VMEM((B, D), bf16),
            pltpu.VMEM((3, 4, 144, 2 * T), bf16),
            pltpu.VMEM((3, 4, 288, T), bf16),
            pltpu.VMEM((3, 4, 288, T), bf16),
            pltpu.VMEM((3, 2, 144, T), bf16),
            pltpu.VMEM((3, 2, 144, T), bf16),
            pltpu.VMEM((3, 2, 144, T), bf16),
            pltpu.VMEM((8, D), f32),
            pltpu.VMEM((8, D), f32),
            pltpu.VMEM((4, 8, D), f32),
            pltpu.VMEM((4, 8, D), f32),
            pltpu.VMEM((4, 8, D), f32),
            dma((3,)),
            dma((32,)), dma((32,)), dma((32,)), dma((32,)),
            dma((9,)), dma((9,)), dma((9,)), dma((9,)),
            dma((36,)), dma((36,)), dma((9,)),
            dma((10,)), dma((10,)),
        ],
        compiler_params=pltpu.CompilerParams(
            collective_id=0, has_side_effects=True, vmem_limit_bytes=62 * 2**20
        ),
        cost_estimate=pl.CostEstimate(flops=33 * 10**9, bytes_accessed=30 * 10**6, transcendentals=0),
    )(
        tokens, cotangent, gain_pre.reshape(1, D), gain_post.reshape(1, D),
        gate_weight, up_weight, down_weight,
    )
    block_out, tokens_grad, pre, post, *rest = outs

    def total(three):
        return (three[0].astype(f32) + three[1].astype(f32)) + three[2].astype(f32)

    return (
        block_out, tokens_grad, pre.reshape(D), post.reshape(D),
        total(rest[3:6]), total(rest[6:9]), total(rest[0:3]),
    )


def solution(mesh):
    in_specs = (
        P(("dp", "tp"), None),
        P(),
        P(),
        P(None, "tp"),
        P(None, "tp"),
        P("tp", None),
        P(("dp", "tp"), None),
    )
    out_specs = (
        P(("dp", "tp"), None),
        P(("dp", "tp"), None),
        P(),
        P(),
        P("dp", "tp"),
        P("dp", "tp"),
        P(("tp", "dp"), None),
    )
    return jax.shard_map(local, mesh=mesh, in_specs=in_specs, out_specs=out_specs, check_vma=False)
```

```python
import jax
import jax.numpy as jnp
from jax import lax
from jax.experimental import pallas as pl
from jax.experimental.pallas import tpu as pltpu
from jax.sharding import PartitionSpec as P

epsilon = 1e-06
root_two_pi = 0.7978845608028654
MESH = pl.DeviceIdType.MESH
D = 2304
F = 1152
B = 32
T = 384
W = 384
f32 = jnp.float32
bf16 = jnp.bfloat16


def gelu_pair(values):
    tanh_arg = root_two_pi * (values + 0.044715 * values * values * values)
    hyper = jnp.tanh(tanh_arg)
    gelu_value = 0.5 * values * (1.0 + hyper)
    gelu_slope = 0.5 * (1.0 + hyper) + 0.5 * values * (1.0 - hyper * hyper) * root_two_pi * (
        1.0 + 3.0 * 0.044715 * values * values
    )
    return (gelu_value, gelu_slope)


def nt(a, b):
    return lax.dot_general(a, b, (((1,), (1,)), ((), ())), preferred_element_type=f32)


def nn(a, b):
    return jnp.dot(a, b, preferred_element_type=f32)


def tile(j, width=T):
    return pl.ds(pl.multiple_of(j * width, 128), width)


def kernel(
    tok, cot, gpre_in, gpost_in, wg_h, wu_h, wd_h,
    bout, tgrad, gain_out, d_own, d_a, g_own, g_a, g_b, u_own, u_a, u_b,
    wg, wu, wd, nbuf, mgbuf, mzbuf, act, us, hown, ht, hz, ntr, part, crecv, xrecv, ysend, yrecv,
    zd, zg, zu, zgf, zuf, gate0, up0, gate1, up1, g_x, g_yz,
    wsem, ag1s, ag1r, ag2s, ag2r, ag3s, ag3r, rs1s, rs1r, rs2s, rs2r, zs, zr, zl, hs, hr, ms, mr, ds, dr, gs, gr,
):
    dp, tp = lax.axis_index("dp"), lax.axis_index("tp")
    c = tp % 2
    x = (tp // 2) % 4
    yh = tp // 8
    yl = dp // 4
    z = dp % 4
    y = yh * 2 + yl

    def dev(dx=0, dy=0, dz=0, dc=0):
        yy = (y + dy) % 4
        return ((yy % 2) * 4 + (z + dz) % 4, ((yy // 2) * 4 + (x + dx) % 4) * 2 + (c + dc) % 2)

    gate_up = ((gate0, up0), (gate1, up1))
    gpre = gpre_in[...].reshape(1, D)
    gpost = gpost_in[...].reshape(1, D)

    loads = [
        pltpu.make_async_copy(h, v, wsem.at[i])
        for i, (h, v) in enumerate(((wg_h, wg), (wu_h, wu), (wd_h, wd)))
    ]
    for load in loads:
        load.start()

    barrier = pltpu.get_barrier_semaphore()
    chips_x = [dict(dx=i, dc=j) for i in range(4) for j in range(2) if i + j]
    chips_yz = [dict(dy=i, dz=j) for i in range(4) for j in range(4) if i + j]
    offs = chips_x + chips_yz
    for o in offs:
        pl.semaphore_signal(barrier, inc=1, device_id=dev(**o), device_id_type=MESH)

    def remote(src, dst, s, r, to):
        return pltpu.make_async_remote_copy(
            src_ref=src, dst_ref=dst, send_sem=s, recv_sem=r, device_id=to, device_id_type=MESH
        )

    def blk(buf, df, ds, core=None):
        dx = df * (1 - c) + ds * c
        dy = df * c + ds * (1 - c)
        xx, yy = (x + dx) % 4, (y + dy) % 4
        return buf.at[yy % 2, yy // 2, xx, c]

    def other_blk(buf, df, ds):
        dx = df * c + ds * (1 - c)
        dy = df * (1 - c) + ds * c
        xx, yy = (x + dx) % 4, (y + dy) % 4
        return buf.at[yy % 2, yy // 2, xx, 1 - c]

    def to_f(sign):
        return dev(dx=(1 - c) * (sign % 4), dy=c * (sign % 4))

    def to_s(sign):
        return dev(dx=c * (sign % 4), dy=(1 - c) * (sign % 4))

    def gather(buf, ss, rr, sent):
        def send(i, ref, to):
            cp = remote(ref, ref, ss.at[i], rr.at[i], to)
            cp.start()
            sent.append(cp)

        def got(i, ref):
            remote(ref, ref, ss.at[i], rr.at[i], dev(dc=1)).wait_recv()

        def core(df, ds):
            send(16 + ds * 4 + df, blk(buf, df, ds), dev(dc=1))

        own = blk(buf, 0, 0)
        send(0, own, to_f(1))
        send(1, own, to_f(-1))
        send(4, own, to_s(1))
        send(8, own, to_s(-1))
        core(0, 0)
        yield
        got(0, blk(buf, 3, 0))
        send(2, blk(buf, 3, 0).at[pl.ds(0, 16)], to_f(1))
        send(7, blk(buf, 3, 0), to_s(1))
        send(11, blk(buf, 3, 0), to_s(-1))
        core(3, 0)
        got(1, blk(buf, 1, 0))
        send(3, blk(buf, 1, 0).at[pl.ds(16, 16)], to_f(-1))
        send(5, blk(buf, 1, 0), to_s(1))
        send(9, blk(buf, 1, 0), to_s(-1))
        core(1, 0)
        yield
        got(2, blk(buf, 2, 0).at[pl.ds(0, 16)])
        got(3, blk(buf, 2, 0).at[pl.ds(16, 16)])
        send(6, blk(buf, 2, 0), to_s(1))
        send(10, blk(buf, 2, 0), to_s(-1))
        core(2, 0)
        yield
        for df, fwd_a, fwd_b in ((0, 12, None), (1, 13, None), (3, None, 14), (2, None, 15)):
            got(4 + df, blk(buf, df, 3))
            if fwd_a is not None:
                send(fwd_a, blk(buf, df, 3), to_s(1))
            core(df, 3)
            got(8 + df, blk(buf, df, 1))
            if fwd_b is not None:
                send(fwd_b, blk(buf, df, 1), to_s(-1))
            core(df, 1)
            yield
        for i, df in ((12, 0), (13, 1), (14, 3), (15, 2)):
            got(i, blk(buf, df, 2))
            core(df, 2)
        yield
        for ds in range(4):
            for df in range(4):
                got(16 + ds * 4 + df, other_blk(buf, df, ds))

    def group_gather(buf, ss, rr, sent):
        def at(dx, dy, core=c):
            yy = (y + dy) % 4
            return buf.at[yy % 2, yy // 2, (x + dx) % 4, core]

        def send(i, ref, **to):
            cp = remote(ref, ref, ss.at[i], rr.at[i], dev(**to))
            cp.start()
            sent.append(cp)

        def got(i, ref):
            remote(ref, ref, ss.at[i], rr.at[i], dev(dc=1)).wait_recv()

        low, high = pl.ds(0, 16), pl.ds(16, 16)
        own = at(0, 0)
        send(0, own, dy=2)
        send(1, own, dx=1)
        send(2, own, dx=3)
        send(5, own, dc=1)
        send(3, own, dy=1)
        send(4, own, dy=3)
        got(0, at(0, 2))
        send(6, at(0, 2), dx=1)
        send(7, at(0, 2), dx=3)
        send(8, at(0, 2), dc=1)
        got(1, at(3, 0))
        send(9, at(3, 0).at[low], dx=1)
        send(12, at(3, 0), dc=1)
        got(2, at(1, 0))
        send(13, at(1, 0).at[high], dx=3)
        send(16, at(1, 0), dc=1)
        for i, dx in ((10, 3), (14, 1)):
            send(i, at(dx, 0), dy=1)
            send(i + 1, at(dx, 0), dy=3)
        got(6, at(3, 2))
        send(20, at(3, 2).at[low], dx=1)
        send(21, at(3, 2), dc=1)
        got(7, at(1, 2))
        send(22, at(1, 2).at[high], dx=3)
        send(23, at(1, 2), dc=1)
        got(9, at(2, 0).at[low])
        got(13, at(2, 0).at[high])
        send(19, at(2, 0), dc=1)
        send(17, at(2, 0), dy=1)
        send(18, at(2, 0), dy=3)
        got(20, at(2, 2).at[low])
        got(22, at(2, 2).at[high])
        send(24, at(2, 2), dc=1)
        for i, dx, dy in ((5, 0, 0), (8, 0, 2), (12, 3, 0), (16, 1, 0), (21, 3, 2), (23, 1, 2), (19, 2, 0), (24, 2, 2)):
            got(i, at(dx, dy, 1 - c))
        yield
        rest = [(i + k, dx, 3 - 2 * k) for i, dx in ((3, 0), (10, 3), (14, 1), (17, 2)) for k in (0, 1)]
        for n, (i, dx, dy) in enumerate(rest):
            got(i, at(dx, dy))
            send(25 + n, at(dx, dy), dc=1)
        yield
        for n, (i, dx, dy) in enumerate(rest):
            got(25 + n, at(dx, dy, 1 - c))

    def run(steps):
        for _ in steps:
            pass

    def core_send(half, i, ss, rr):
        cp = remote(part.at[half, :, 1 - c], crecv.at[i], ss.at[i], rr.at[i], dev(dc=1))
        cp.start()
        return cp

    def core_add(half, i, ss, rr):
        remote(crecv.at[i], crecv.at[i], ss.at[i], rr.at[i], dev(dc=1)).wait_recv()

        def one(k, _):
            part[half, k, c] = (part[half, k, c].astype(f32) + crecv[i, k].astype(f32)).astype(bf16)
            return 0

        lax.fori_loop(0, 4, one, 0)

    def x_send(half, i, ss, rr):
        out = []
        for dx in (2, 1, 3):
            k = 2 + i * 3 + dx - 1
            cp = remote(
                part.at[half, (x + dx) % 4, c], xrecv.at[i, dx - 1], ss.at[k], rr.at[k], dev(dx=dx)
            )
            cp.start()
            out.append(cp)
        return out

    def x_sum(half, i, ss, rr):
        for dx in (1, 3, 2):
            k = 2 + i * 3 + dx - 1
            ref = xrecv.at[i, dx - 1]
            remote(ref, ref, ss.at[k], rr.at[k], dev(dx=dx)).wait_recv()
        total = part[half, x, c].astype(f32)
        for dx in (1, 3, 2):
            total = total + xrecv[i, dx - 1].astype(f32)
        return total

    def y_send(total, ss, rr):
        ysend[...] = total.astype(bf16)
        cp = remote(ysend, yrecv, ss.at[8], rr.at[8], dev(dy=2))
        cp.start()
        return cp

    def y_sum(total, ss, rr):
        remote(yrecv, yrecv, ss.at[8], rr.at[8], dev(dy=2)).wait_recv()
        return total + yrecv[...].astype(f32)

    tok_f = tok[...].astype(f32)
    recip_in = lax.rsqrt(jnp.mean(tok_f * tok_f, axis=-1, keepdims=True) + epsilon)
    nbuf[yl, yh, x, c] = (tok_f * recip_in * gpre).astype(bf16)

    pl.semaphore_wait(barrier, len(offs))
    sent1 = []
    steps = group_gather(nbuf, ag1s, ag1r, sent1)
    next(steps)
    for load in loads:
        load.wait()

    def forward(a, b, is_own):
        rows = nbuf[a, b].reshape(256, D)
        for j in range(4):
            if j < 3:
                gate_up[j % 2][0][...] = nn(rows, wg[:, pl.ds(j * T, T)])
                gate_up[j % 2][1][...] = nn(rows, wu[:, pl.ds(j * T, T)])
            if j > 0:
                cols = pl.ds((j - 1) * T, T)
                up = gate_up[(j - 1) % 2][1][...]
                value, slope = gelu_pair(gate_up[(j - 1) % 2][0][...])
                hidden = (value * up).astype(bf16)
                act[a, b, :, cols] = value.astype(bf16)
                us[a, b, :, cols] = (up * slope).astype(bf16)
                if is_own:
                    hown[b, :, cols] = hidden
                ht[cols, tile(a * 2 + b, 256)] = hidden.T

    def down(half):
        def one(j, _):
            part[half, :, :, :, tile(j)] = (
                nn(hown[half], wd[:, tile(j)]).astype(bf16).reshape(4, 2, B, T)
            )
            return 0

        lax.fori_loop(0, 6, one, 0)

    forward(yl, 1 - yh, True)
    down(1 - yh)
    pend = [core_send(1 - yh, 0, rs1s, rs1r)]
    forward(yl, yh, True)
    core_add(1 - yh, 0, rs1s, rs1r)
    pend += x_send(1 - yh, 0, rs1s, rs1r)
    down(yh)
    pend.append(core_send(yh, 1, rs1s, rs1r))
    next(steps)
    core_add(yh, 1, rs1s, rs1r)
    pend += x_send(yh, 1, rs1s, rs1r)
    run(steps)
    forward(1 - yl, 0, False)
    pend.append(y_send(x_sum(1 - yh, 0, rs1s, rs1r), rs1s, rs1r))
    forward(1 - yl, 1, False)

    sent2 = []
    near = (z + 1 - 2 * (z % 2), 3 - z)
    step = (1 + 2 * (z % 2), 3 - 2 * (z % 2))

    def shards(q):
        flip = q + 1 - 2 * (q % 2)
        return ((q, 3 - q), (q, flip))

    def ht_rows(q):
        return pl.ds(pl.multiple_of((yl * 4 + q) * 144, 16), 144)

    for h in range(2):
        for i in range(2):
            cp = remote(ht.at[ht_rows(shards(near[h])[h][i])], hz.at[h, i], hs.at[h * 2 + i], hr.at[h * 2 + i], dev(dz=step[h]))
            cp.start()
            sent2.append(cp)

    mixed = y_sum(x_sum(yh, 1, rs1s, rs1r), rs1s, rs1r)

    recip_mix = lax.rsqrt(jnp.mean(mixed * mixed, axis=-1, keepdims=True) + epsilon)
    scaled_mix = mixed * recip_mix
    cot_f = cot[...].astype(f32)
    weighted = cot_f * gpost
    mix_grad = recip_mix * (
        weighted - scaled_mix * jnp.mean(weighted * scaled_mix, axis=-1, keepdims=True)
    )
    mgbuf[yl, yh, x, c] = mix_grad.astype(bf16)
    bout[...] = (tok[...].astype(f32) + scaled_mix * gpost).astype(bf16)
    g_x[x * 2 + c, 1:2, :] = jnp.sum(cot_f * scaled_mix, axis=0, keepdims=True)
    for cp in pend + sent1:
        cp.wait_send()

    def mz_half(h):
        return (pl.ds(0, B), pl.ds(h * F, F))

    for h in range(2):
        cp = remote(
            mgbuf.at[yl, yh, x, c].at[mz_half(h)], mzbuf.at[yl, yh, x, c].at[mz_half(h)], ms.at[h], mr.at[h], dev(dz=step[h])
        )
        cp.start()
        sent2.append(cp)
    run(gather(mgbuf, ag2s, ag2r, sent2))

    def turn(k, _):
        def one(j, _):
            cols = pl.ds(pl.multiple_of(yl * F + j * T, 128), T)
            ntr[tile(j), tile(k, 256)] = nbuf[k // 2, k % 2, :, :, :, cols].reshape(256, T).T
            return 0

        lax.fori_loop(0, 3, one, 0)
        return 0

    lax.fori_loop(0, 4, turn, 0)

    units = {}
    sent3 = []

    bufs = {"g": (zg, zgf, g_own, g_a, g_b, 0), "u": (zu, zuf, u_own, u_a, u_b, 3)}

    def z_first(kind, j):
        buf, fwd, own, _, _, base = bufs[kind]
        q = (base + j) * 4
        for k, dz in ((0, 1), (1, 3)):
            cp = remote(
                buf.at[j, (z + 2) % 4].at[pl.ds(k * 144, 144)], fwd.at[j, k], zs.at[q + k], zr.at[q + k], dev(dz=dz)
            )
            cp.start()
            sent3.append(cp)
        cp = pltpu.make_async_copy(buf.at[j, z], own.at[:, pl.ds(j * T, T)], zl.at[base + j])
        cp.start()
        units[kind, j] = cp

    def z_second(kind, j):
        buf, fwd, _, out_a, out_b, base = bufs[kind]
        q = (base + j) * 4
        for k, dz, out in ((0, 1, out_a), (1, 3, out_b)):
            ref = fwd.at[j, k]
            remote(ref, ref, zs.at[q + k], zr.at[q + k], dev(dz=dz)).wait_recv()
            to = (z + dz) % 4
            rows = pl.ds(k * 144, 144)
            buf[j, to, rows] = (buf[j, to, rows].astype(f32) + fwd[j, k].astype(f32)).astype(bf16)
            cp = remote(
                buf.at[j, to], out.at[:, pl.ds(j * T, T)], zs.at[q + 2 + k], zr.at[q + 2 + k], dev(dz=dz)
            )
            cp.start()
            sent3.append(cp)

    def down_grad(h):
        for i in range(2):
            ref = hz.at[h, i]
            remote(ref, ref, hs.at[h * 2 + i], hr.at[h * 2 + i], dev(dz=step[h])).wait_recv()
        mine = shards(z)[h]
        for i in range(2):

            def one(j, _, i=i):
                cols = pl.ds(pl.multiple_of(h * F + j * T, 128), T)
                total = nn(ht[ht_rows(mine[i]), :], mgbuf[:, :, :, :, :, cols].reshape(1024, T))
                total = total + nn(hz[h, i], mzbuf[:, :, :, :, :, cols].reshape(1024, T))
                zd[h, i, :, tile(j)] = total.astype(bf16)
                return 0

            lax.fori_loop(0, 3, one, 0)
        cp = remote(zd.at[h, 1], d_a.at[:, pl.ds(h * F, F)], ds.at[h], dr.at[h], dev(dz=step[1 - h]))
        cp.start()
        sent3.append(cp)
        cp = pltpu.make_async_copy(zd.at[h, 0], d_own.at[:, pl.ds(h * F, F)], zl.at[6 + h])
        cp.start()
        units["d", h] = cp

    def hidden_grad(j):
        def one(k, _):
            a, b = k // 2, k % 2
            grad = nt(mgbuf[a, b].reshape(256, D), wd[pl.ds(j * T, T), :])
            cols = pl.ds(j * T, T)
            act[a, b, :, cols] = (grad * act[a, b, :, cols].astype(f32)).astype(bf16)
            us[a, b, :, cols] = (grad * us[a, b, :, cols].astype(f32)).astype(bf16)
            return 0

        lax.fori_loop(0, 4, one, 0)

    def in_grad(buf, src, j):
        def one(i, _):
            rhs = src[:, :, :, pl.ds(j * T, T)].reshape(1024, T)
            lhs = ntr[pl.ds(pl.multiple_of(i * 288, 32), 288), :]
            buf[j, i] = nn(lhs, rhs).astype(bf16)
            return 0

        lax.fori_loop(0, 4, one, 0)

    for h in range(2):
        ref = mzbuf.at[yl, yh, x, c].at[mz_half(h)]
        remote(ref, ref, ms.at[h], mr.at[h], dev(dz=step[h])).wait_recv()
    steps = gather(mzbuf, ag3s, ag3r, sent2)
    next(steps)
    for j in range(3):
        hidden_grad(j)
        next(steps, None)
        in_grad(zg, us, j)
        z_first("g", j)
        next(steps, None)
        if j >= 1:
            z_second("g", j - 1)
        in_grad(zu, act, j)
        z_first("u", j)
        next(steps, None)
        if j >= 1:
            z_second("u", j - 1)

    def normed_grad(half):
        def one(j, _):
            total = nt(us[yl, half], wg[tile(j), :]) + nt(act[yl, half], wu[tile(j), :])
            part[half, :, :, :, tile(j)] = total.astype(bf16).reshape(4, 2, B, T)
            return 0

        lax.fori_loop(0, 6, one, 0)

    normed_grad(1 - yh)
    pend = [core_send(1 - yh, 0, rs2s, rs2r)]
    next(steps, None)
    normed_grad(yh)
    pend.append(core_send(yh, 1, rs2s, rs2r))
    core_add(1 - yh, 0, rs2s, rs2r)
    pend += x_send(1 - yh, 0, rs2s, rs2r)
    next(steps, None)
    core_add(yh, 1, rs2s, rs2r)
    pend += x_send(yh, 1, rs2s, rs2r)
    z_second("g", 2)
    run(steps)
    down_grad(0)
    pend.append(y_send(x_sum(1 - yh, 0, rs2s, rs2r), rs2s, rs2r))
    z_second("u", 2)
    down_grad(1)
    grad_in = y_sum(x_sum(yh, 1, rs2s, rs2r), rs2s, rs2r)
    tok_f = tok[...].astype(f32)
    recip_in = lax.rsqrt(jnp.mean(tok_f * tok_f, axis=-1, keepdims=True) + epsilon)
    scaled_in = tok_f * recip_in
    weighted = grad_in * gpre
    back = recip_in * (weighted - scaled_in * jnp.mean(weighted * scaled_in, axis=-1, keepdims=True))
    tgrad[...] = (cot[...].astype(f32) + back).astype(bf16)
    g_x[x * 2 + c, 0:1, :] = jnp.sum(grad_in * scaled_in, axis=0, keepdims=True)

    def exchange(slots, me, peers, base, place):
        cps = []
        for n, o in enumerate(peers):
            cp = remote(slots.at[me], slots.at[me], gs.at[base + n], gr.at[base + n], dev(**o))
            cp.start()
            cps.append(cp)
        for n, o in enumerate(peers):
            ref = slots.at[place({k: -v for k, v in o.items()})]
            remote(ref, ref, gs.at[base + n], gr.at[base + n], dev(**o)).wait_recv()
        value = slots[0]
        for n in range(1, len(peers) + 1):
            value = value + slots[n]
        return value, cps

    value, cps = exchange(
        g_x, x * 2 + c, chips_x, 0, lambda o: ((x + o["dx"] + 4) % 4) * 2 + (c + o["dc"] + 2) % 2
    )
    sent3 += cps
    g_yz[y * 4 + z] = value
    value, cps = exchange(
        g_yz, y * 4 + z, chips_yz, 7, lambda o: ((y + o["dy"] + 4) % 4) * 4 + (z + o["dz"] + 4) % 4
    )
    sent3 += cps
    gain_out[...] = value

    for kind in "gu":
        _, _, own, out_a, out_b, base = bufs[kind]
        for j in range(3):
            q = (base + j) * 4
            for k, out in ((0, out_a), (1, out_b)):
                ref = out.at[:, pl.ds(j * T, T)]
                remote(ref, ref, zs.at[q + 2 + k], zr.at[q + 2 + k], dev(dz=1)).wait_recv()
            units[kind, j].wait()
    for h in range(2):
        ref = d_a.at[:, pl.ds(h * F, F)]
        remote(ref, ref, ds.at[h], dr.at[h], dev(dz=1)).wait_recv()
        units["d", h].wait()
    for cp in pend + sent2 + sent3:
        cp.wait_send()


def finish(
    bout, tgrad, gains, d_own, d_a, g_own, g_a, g_b, u_own, u_a, u_b,
    bout_out, tgrad_out, pre_out, post_out, gate_out, up_out, down_out,
):
    bout_out[...] = bout[...]
    tgrad_out[...] = tgrad[...]
    pre_out[...] = gains[0, :]
    post_out[...] = gains[1, :]
    gate_out[...] = (g_own[...].astype(f32) + g_a[...].astype(f32)) + g_b[...].astype(f32)
    up_out[...] = (u_own[...].astype(f32) + u_a[...].astype(f32)) + u_b[...].astype(f32)
    down_out[...] = d_own[...].astype(f32) + d_a[...].astype(f32)


def local(tokens, gain_pre, gain_post, gate_weight, up_weight, down_weight, cotangent):
    vm = pl.BlockSpec(memory_space=pltpu.VMEM)
    hbm = pl.BlockSpec(memory_space=pl.ANY)
    S = jax.ShapeDtypeStruct
    dma = pltpu.SemaphoreType.DMA
    V = pltpu.VMEM
    outs = pl.pallas_call(
        kernel,
        out_shape=(
            [S((B, D), bf16), S((B, D), bf16), S((2, D), f32)]
            + [S((144, D), bf16)] * 2
            + [S((288, F), bf16)] * 6
        ),
        in_specs=[vm] * 4 + [hbm] * 3,
        out_specs=[vm] * 3 + [hbm] * 8,
        scratch_shapes=[
            V((D, F), bf16),
            V((D, F), bf16),
            V((F, D), bf16),
            V((2, 2, 4, 2, B, D), bf16),
            V((2, 2, 4, 2, B, D), bf16),
            V((2, 2, 4, 2, B, D), bf16),
            V((2, 2, 256, F), bf16),
            V((2, 2, 256, F), bf16),
            V((2, 256, F), bf16),
            V((F, 1024), bf16),
            V((2, 2, 144, 1024), bf16),
            V((F, 1024), bf16),
            V((2, 4, 2, B, D), bf16),
            V((2, 4, B, D), bf16),
            V((2, 3, B, D), bf16),
            V((B, D), bf16),
            V((B, D), bf16),
            V((2, 2, 144, F), bf16),
            V((3, 4, 288, T), bf16),
            V((3, 4, 288, T), bf16),
            V((3, 2, 144, T), bf16),
            V((3, 2, 144, T), bf16),
            V((256, T), f32),
            V((256, T), f32),
            V((256, T), f32),
            V((256, T), f32),
            V((8, 2, D), f32),
            V((16, 2, D), f32),
            dma((3,)),
            dma((33,)), dma((33,)), dma((32,)), dma((32,)), dma((32,)), dma((32,)),
            dma((9,)), dma((9,)), dma((9,)), dma((9,)),
            dma((24,)), dma((24,)), dma((8,)),
            dma((4,)), dma((4,)), dma((2,)), dma((2,)), dma((2,)), dma((2,)),
            dma((22,)), dma((22,)),
        ],
        compiler_params=pltpu.CompilerParams(
            collective_id=0, has_side_effects=True, vmem_limit_bytes=63 * 2**20
        ),
        cost_estimate=pl.CostEstimate(flops=33 * 10**9, bytes_accessed=30 * 10**6, transcendentals=0),
    )(
        tokens, cotangent, gain_pre, gain_post,
        gate_weight, up_weight, down_weight,
    )

    def whole(*shape):
        return pl.BlockSpec(shape, lambda i: (0,) * len(shape))

    def rows(n, width):
        return pl.BlockSpec((n, width), lambda i: (i, 0))

    n = 3
    return pl.pallas_call(
        finish,
        grid=(n,),
        out_shape=[
            S((B, D), bf16), S((B, D), bf16), S((D,), f32), S((D,), f32),
            S((288, F), f32), S((288, F), f32), S((144, D), f32),
        ],
        in_specs=[whole(B, D), whole(B, D), whole(2, D)] + [rows(144 // n, D)] * 2 + [rows(288 // n, F)] * 6,
        out_specs=[whole(B, D), whole(B, D), whole(D), whole(D)]
        + [rows(288 // n, F)] * 2 + [rows(144 // n, D)],
    )(*outs)


def solution(mesh):
    in_specs = (
        P(("dp", "tp"), None),
        P(),
        P(),
        P(None, "tp"),
        P(None, "tp"),
        P("tp", None),
        P(("dp", "tp"), None),
    )
    out_specs = (
        P(("dp", "tp"), None),
        P(("dp", "tp"), None),
        P(),
        P(),
        P("dp", "tp"),
        P("dp", "tp"),
        P(("tp", "dp"), None),
    )
    return jax.shard_map(local, mesh=mesh, in_specs=in_specs, out_specs=out_specs, check_vma=False)
```

```python
import jax
import jax.numpy as jnp
from jax import lax
from jax.experimental import pallas as pl
from jax.experimental.pallas import tpu as pltpu
from jax.sharding import PartitionSpec as P

epsilon = 1e-06
root_two_pi = 0.7978845608028654
MESH = pl.DeviceIdType.MESH
D = 2304
F = 1152
B = 32
T = 384
f32 = jnp.float32
bf16 = jnp.bfloat16


def gelu_pair(values):
    tanh_arg = root_two_pi * (values + 0.044715 * values * values * values)
    hyper = jnp.tanh(tanh_arg)
    gelu_value = 0.5 * values * (1.0 + hyper)
    gelu_slope = 0.5 * (1.0 + hyper) + 0.5 * values * (1.0 - hyper * hyper) * root_two_pi * (
        1.0 + 3.0 * 0.044715 * values * values
    )
    return (gelu_value, gelu_slope)


def nt(a, b):
    return lax.dot_general(a, b, (((1,), (1,)), ((), ())), preferred_element_type=f32)


def nn(a, b):
    return jnp.dot(a, b, preferred_element_type=f32)


def tile(j, width=T):
    return pl.ds(pl.multiple_of(j * width, 128), width)


def kernel(
    tok, cot, gpre_in, gpost_in, wg_h, wu_h, wd_h,
    bout, tgrad, gain_out, d_own, d_a, g_own, g_a, g_b, u_own, u_a, u_b,
    wgu, wd, nbuf, mgbuf, mzbuf, au, hown, ht, hz, ntr, part, crecv, xrecv, ysend, yrecv, yall,
    zd, zg, zu, zgf, zuf, gu0, gu1, g_x, g_yz,
    wsem, ag1s, ag1r, ag2s, ag2r, ag3s, ag3r, rs1s, rs1r, rs2s, rs2r, zs, zr, zl, hs, hr, ms, mr, ds, dr, gs, gr,
):
    dp, tp = lax.axis_index("dp"), lax.axis_index("tp")
    c = tp % 2
    x = (tp // 2) % 4
    yh = tp // 8
    yl = dp // 4
    z = dp % 4
    y = yh * 2 + yl

    def dev(dx=0, dy=0, dz=0, dc=0):
        yy = (y + dy) % 4
        return ((yy % 2) * 4 + (z + dz) % 4, ((yy // 2) * 4 + (x + dx) % 4) * 2 + (c + dc) % 2)

    gate_up = (gu0, gu1)
    gpre = gpre_in[...].reshape(1, D)
    gpost = gpost_in[...].reshape(1, D)

    loads = [
        pltpu.make_async_copy(
            h.at[:, pl.ds(j * T, T)], wgu.at[:, pl.ds((2 * j + k) * T, T)], wsem.at[2 * j + k]
        )
        for j in range(3)
        for k, h in enumerate((wg_h, wu_h))
    ] + [pltpu.make_async_copy(wd_h, wd, wsem.at[6])]

    barrier = pltpu.get_barrier_semaphore()
    chips_x = [dict(dx=i, dc=j) for i in range(4) for j in range(2) if i + j]
    chips_yz = [dict(dy=i, dz=j) for i in range(4) for j in range(4) if i + j]
    offs = chips_x + chips_yz
    for o in offs:
        pl.semaphore_signal(barrier, inc=1, device_id=dev(**o), device_id_type=MESH)

    def remote(src, dst, s, r, to):
        return pltpu.make_async_remote_copy(
            src_ref=src, dst_ref=dst, send_sem=s, recv_sem=r, device_id=to, device_id_type=MESH
        )

    def blk(buf, df, ds, core=None):
        dx = df * (1 - c) + ds * c
        dy = df * c + ds * (1 - c)
        xx, yy = (x + dx) % 4, (y + dy) % 4
        return buf.at[yy % 2, yy // 2, xx, c]

    def other_blk(buf, df, ds):
        dx = df * c + ds * (1 - c)
        dy = df * (1 - c) + ds * c
        xx, yy = (x + dx) % 4, (y + dy) % 4
        return buf.at[yy % 2, yy // 2, xx, 1 - c]

    def to_f(sign):
        return dev(dx=(1 - c) * (sign % 4), dy=c * (sign % 4))

    def to_s(sign):
        return dev(dx=c * (sign % 4), dy=(1 - c) * (sign % 4))

    def gather(buf, ss, rr, sent):
        def send(i, ref, to):
            cp = remote(ref, ref, ss.at[i], rr.at[i], to)
            cp.start()
            sent.append(cp)

        def got(i, ref):
            remote(ref, ref, ss.at[i], rr.at[i], dev(dc=1)).wait_recv()

        def core(df, ds):
            send(16 + ds * 4 + df, blk(buf, df, ds), dev(dc=1))

        own = blk(buf, 0, 0)
        send(0, own, to_f(1))
        send(1, own, to_f(-1))
        send(4, own, to_s(1))
        send(8, own, to_s(-1))
        core(0, 0)
        yield
        got(0, blk(buf, 3, 0))
        send(2, blk(buf, 3, 0).at[pl.ds(0, 16)], to_f(1))
        send(7, blk(buf, 3, 0), to_s(1))
        send(11, blk(buf, 3, 0), to_s(-1))
        core(3, 0)
        got(1, blk(buf, 1, 0))
        send(3, blk(buf, 1, 0).at[pl.ds(16, 16)], to_f(-1))
        send(5, blk(buf, 1, 0), to_s(1))
        send(9, blk(buf, 1, 0), to_s(-1))
        core(1, 0)
        yield
        got(2, blk(buf, 2, 0).at[pl.ds(0, 16)])
        got(3, blk(buf, 2, 0).at[pl.ds(16, 16)])
        send(6, blk(buf, 2, 0), to_s(1))
        send(10, blk(buf, 2, 0), to_s(-1))
        core(2, 0)
        yield
        for df, fwd_a, fwd_b in ((0, 12, None), (1, 13, None), (3, None, 14), (2, None, 15)):
            got(4 + df, blk(buf, df, 3))
            if fwd_a is not None:
                send(fwd_a, blk(buf, df, 3), to_s(1))
            core(df, 3)
            got(8 + df, blk(buf, df, 1))
            if fwd_b is not None:
                send(fwd_b, blk(buf, df, 1), to_s(-1))
            core(df, 1)
            yield
        for i, df in ((12, 0), (13, 1), (14, 3), (15, 2)):
            got(i, blk(buf, df, 2))
            core(df, 2)
        yield
        for ds in range(4):
            for df in range(4):
                got(16 + ds * 4 + df, other_blk(buf, df, ds))

    def group_gather(buf, ss, rr, sent):
        def at(dx, dy, core=c):
            yy = (y + dy) % 4
            return buf.at[yy % 2, yy // 2, (x + dx) % 4, core]

        def send(i, ref, **to):
            cp = remote(ref, ref, ss.at[i], rr.at[i], dev(**to))
            cp.start()
            sent.append(cp)

        def got(i, ref):
            remote(ref, ref, ss.at[i], rr.at[i], dev(dc=1)).wait_recv()

        low, high = pl.ds(0, 16), pl.ds(16, 16)
        own = at(0, 0)
        send(0, own, dy=2)
        send(1, own, dx=1)
        send(2, own, dx=3)
        send(5, own, dc=1)
        yield
        got(0, at(0, 2))
        send(6, at(0, 2), dx=1)
        send(7, at(0, 2), dx=3)
        send(8, at(0, 2), dc=1)
        send(3, own, dy=1)
        send(4, own, dy=3)
        yield
        got(1, at(3, 0))
        send(9, at(3, 0).at[low], dx=1)
        send(12, at(3, 0), dc=1)
        got(2, at(1, 0))
        send(13, at(1, 0).at[high], dx=3)
        send(16, at(1, 0), dc=1)
        for i, dx in ((10, 3), (14, 1)):
            send(i, at(dx, 0), dy=1)
            send(i + 1, at(dx, 0), dy=3)
        yield
        got(6, at(3, 2))
        send(20, at(3, 2).at[low], dx=1)
        send(21, at(3, 2), dc=1)
        got(7, at(1, 2))
        send(22, at(1, 2).at[high], dx=3)
        send(23, at(1, 2), dc=1)
        got(9, at(2, 0).at[low])
        got(13, at(2, 0).at[high])
        send(19, at(2, 0), dc=1)
        send(17, at(2, 0), dy=1)
        send(18, at(2, 0), dy=3)
        got(20, at(2, 2).at[low])
        got(22, at(2, 2).at[high])
        send(24, at(2, 2), dc=1)
        for i, dx, dy in ((5, 0, 0), (8, 0, 2), (12, 3, 0), (16, 1, 0), (21, 3, 2), (23, 1, 2), (19, 2, 0), (24, 2, 2)):
            got(i, at(dx, dy, 1 - c))
        yield
        rest = [(i + k, dx, 3 - 2 * k) for i, dx in ((3, 0), (10, 3), (14, 1), (17, 2)) for k in (0, 1)]
        for n, (i, dx, dy) in enumerate(rest):
            got(i, at(dx, dy))
            send(25 + n, at(dx, dy), dc=1)
        yield
        for n, (i, dx, dy) in enumerate(rest):
            got(25 + n, at(dx, dy, 1 - c))

    def run(steps):
        for _ in steps:
            pass

    def core_send(half, i, ss, rr):
        cp = remote(part.at[half, :, 1 - c], crecv.at[i], ss.at[i], rr.at[i], dev(dc=1))
        cp.start()
        return cp

    def core_add(half, i, ss, rr):
        remote(crecv.at[i], crecv.at[i], ss.at[i], rr.at[i], dev(dc=1)).wait_recv()

        def one(k, _):
            part[half, k, c] = (part[half, k, c].astype(f32) + crecv[i, k].astype(f32)).astype(bf16)
            return 0

        lax.fori_loop(0, 4, one, 0)

    def x_copies(half, i, ss, rr):
        out = []
        for dx in (2, 1, 3):
            k = 2 + i * 3 + dx - 1
            out.append(remote(
                part.at[half, (x + dx) % 4, c], xrecv.at[i, dx - 1], ss.at[k], rr.at[k], dev(dx=dx)
            ))
        return out

    def x_sum(half, i, ss, rr):
        for dx in (1, 3, 2):
            k = 2 + i * 3 + dx - 1
            ref = xrecv.at[i, dx - 1]
            remote(ref, ref, ss.at[k], rr.at[k], dev(dx=dx)).wait_recv()
        total = part[half, x, c].astype(f32)
        for dx in (1, 3, 2):
            total = total + xrecv[i, dx - 1].astype(f32)
        return total

    def y_copy(ss, rr):
        return remote(ysend, yrecv, ss.at[8], rr.at[8], dev(dy=2))

    def y_copy_all(ss, rr):
        return remote(part.at[1 - yh, :, c], yall, ss.at[8], rr.at[8], dev(dy=2))

    def start(copies):
        for cp in copies:
            cp.start()

    def sum_first(ss, rr):
        core_add(1 - yh, 0, ss, rr)

        @pl.when(c == 0)
        def _():
            start(x_copies(1 - yh, 0, ss, rr))

        @pl.when(c == 1)
        def _():
            start([y_copy_all(ss, rr)])

    def sum_second(ss, rr):
        core_add(yh, 1, ss, rr)

        @pl.when(c == 0)
        def _():
            start(x_copies(yh, 1, ss, rr))

    def sum_third(ss, rr):
        @pl.when(c == 0)
        def _():
            ysend[...] = x_sum(1 - yh, 0, ss, rr).astype(bf16)
            start([y_copy(ss, rr)])

        @pl.when(c == 1)
        def _():
            y_copy_all(ss, rr).wait_recv()

            def one(k, _):
                part[yh, k, c] = (part[yh, k, c].astype(f32) + yall[k].astype(f32)).astype(bf16)
                return 0

            lax.fori_loop(0, 4, one, 0)
            start(x_copies(yh, 1, ss, rr))

    def sum_last(ss, rr):
        total = x_sum(yh, 1, ss, rr)

        @pl.when(c == 0)
        def _():
            y_copy(ss, rr).wait_recv()

        return total + yrecv[...].astype(f32)

    def sum_wait(ss, rr):
        @pl.when(c == 0)
        def _():
            for cp in x_copies(1 - yh, 0, ss, rr) + [y_copy(ss, rr)]:
                cp.wait_send()

        @pl.when(c == 1)
        def _():
            y_copy_all(ss, rr).wait_send()

        for cp in x_copies(yh, 1, ss, rr):
            cp.wait_send()

    @pl.when(c == 1)
    def _():
        yrecv[...] = jnp.zeros_like(yrecv)

    tok_f = tok[...].astype(f32)
    recip_in = lax.rsqrt(jnp.mean(tok_f * tok_f, axis=-1, keepdims=True) + epsilon)
    nbuf[yl, yh, x, c] = (tok_f * recip_in * gpre).astype(bf16)

    pl.semaphore_wait(barrier, len(offs))
    sent1 = []
    steps = group_gather(nbuf, ag1s, ag1r, sent1)
    for some in (loads[0:2], loads[2:4], loads[4:7]):
        next(steps)
        for load in some:
            load.start()
    next(steps)
    for load in loads:
        load.wait()

    def forward(a, b, is_own, between=None):
        rows = nbuf[a, b].reshape(256, D)
        for j in range(4):
            if j < 3:
                gate_up[j % 2][...] = nn(rows, wgu[:, pl.ds(j * 2 * T, 2 * T)])
            if j > 0:
                cols = pl.ds((j - 1) * T, T)
                up = gate_up[(j - 1) % 2][:, T:]
                value, slope = gelu_pair(gate_up[(j - 1) % 2][:, :T])
                hidden = (value * up).astype(bf16)
                au[a, b, :, pl.ds((j - 1) * 2 * T, T)] = (up * slope).astype(bf16)
                au[a, b, :, pl.ds((j - 1) * 2 * T + T, T)] = value.astype(bf16)
                if is_own:
                    hown[b, :, cols] = hidden
                ht[cols, tile(a * 2 + b, 256)] = hidden.T
            if between is not None and j == 1:
                between()

    def down(half):
        def one(j, _):
            part[half, :, :, :, tile(j, 2 * T)] = (
                nn(hown[half], wd[:, tile(j, 2 * T)]).astype(bf16).reshape(4, 2, B, 2 * T)
            )
            return 0

        lax.fori_loop(0, 3, one, 0)

    forward(yl, 1 - yh, True)
    down(1 - yh)
    pend = [core_send(1 - yh, 0, rs1s, rs1r)]

    forward(yl, yh, True, lambda: sum_first(rs1s, rs1r))
    down(yh)
    pend.append(core_send(yh, 1, rs1s, rs1r))
    next(steps)
    sum_second(rs1s, rs1r)
    run(steps)
    forward(1 - yl, 0, False)
    sum_third(rs1s, rs1r)
    forward(1 - yl, 1, False)

    sent2 = []
    near = (z + 1 - 2 * (z % 2), 3 - z)
    step = (1 + 2 * (z % 2), 3 - 2 * (z % 2))

    def shards(q):
        flip = q + 1 - 2 * (q % 2)
        return ((q, 3 - q), (q, flip))

    def ht_rows(q):
        return pl.ds(pl.multiple_of((yl * 4 + q) * 144, 16), 144)

    for h in range(2):
        for i in range(2):
            cp = remote(ht.at[ht_rows(shards(near[h])[h][i])], hz.at[h, i], hs.at[h * 2 + i], hr.at[h * 2 + i], dev(dz=step[h]))
            cp.start()
            sent2.append(cp)

    mixed = sum_last(rs1s, rs1r)

    recip_mix = lax.rsqrt(jnp.mean(mixed * mixed, axis=-1, keepdims=True) + epsilon)
    scaled_mix = mixed * recip_mix
    cot_f = cot[...].astype(f32)
    weighted = cot_f * gpost
    mix_grad = recip_mix * (
        weighted - scaled_mix * jnp.mean(weighted * scaled_mix, axis=-1, keepdims=True)
    )
    mgbuf[yl, yh, x, c] = mix_grad.astype(bf16)
    bout[...] = (tok[...].astype(f32) + scaled_mix * gpost).astype(bf16)
    g_x[x * 2 + c, 1:2, :] = jnp.sum(cot_f * scaled_mix, axis=0, keepdims=True)
    for cp in pend + sent1:
        cp.wait_send()
    sum_wait(rs1s, rs1r)

    def mz_half(h):
        return (pl.ds(0, B), pl.ds(h * F, F))

    for h in range(2):
        cp = remote(
            mgbuf.at[yl, yh, x, c].at[mz_half(h)], mzbuf.at[yl, yh, x, c].at[mz_half(h)], ms.at[h], mr.at[h], dev(dz=step[h])
        )
        cp.start()
        sent2.append(cp)
    run(gather(mgbuf, ag2s, ag2r, sent2))

    def turn(k, _):
        def one(j, _):
            cols = pl.ds(pl.multiple_of(yl * F + j * T, 128), T)
            ntr[tile(j), tile(k, 256)] = nbuf[k // 2, k % 2, :, :, :, cols].reshape(256, T).T
            return 0

        lax.fori_loop(0, 3, one, 0)
        return 0

    lax.fori_loop(0, 4, turn, 0)

    units = {}
    sent3 = []

    bufs = {"g": (zg, zgf, g_own, g_a, g_b, 0), "u": (zu, zuf, u_own, u_a, u_b, 3)}

    def z_first(kind, j):
        buf, fwd, own, _, _, base = bufs[kind]
        q = (base + j) * 4
        for k, dz in ((0, 1), (1, 3)):
            cp = remote(
                buf.at[j, (z + 2) % 4].at[pl.ds(k * 144, 144)], fwd.at[j, k], zs.at[q + k], zr.at[q + k], dev(dz=dz)
            )
            cp.start()
            sent3.append(cp)

    def z_own(kind, j):
        buf, _, own, _, _, base = bufs[kind]
        cp = pltpu.make_async_copy(buf.at[j, z], own.at[:, pl.ds(j * T, T)], zl.at[base + j])
        cp.start()
        units[kind, j] = cp

    def z_second(kind, j):
        buf, fwd, _, out_a, out_b, base = bufs[kind]
        q = (base + j) * 4
        for k, dz, out in ((0, 1, out_a), (1, 3, out_b)):
            ref = fwd.at[j, k]
            remote(ref, ref, zs.at[q + k], zr.at[q + k], dev(dz=dz)).wait_recv()
            to = (z + dz) % 4
            rows = pl.ds(k * 144, 144)
            buf[j, to, rows] = (buf[j, to, rows].astype(f32) + fwd[j, k].astype(f32)).astype(bf16)
            cp = remote(
                buf.at[j, to], out.at[:, pl.ds(j * T, T)], zs.at[q + 2 + k], zr.at[q + 2 + k], dev(dz=dz)
            )
            cp.start()
            sent3.append(cp)

    def down_grad(h):
        for i in range(2):
            ref = hz.at[h, i]
            remote(ref, ref, hs.at[h * 2 + i], hr.at[h * 2 + i], dev(dz=step[h])).wait_recv()
        mine = shards(z)[h]
        for i in range(2):
            for at, width in ((0, 2 * T), (2 * T, T)):
                cols = pl.ds(h * F + at, width)
                total = nn(ht[ht_rows(mine[i]), :], mgbuf[:, :, :, :, :, cols].reshape(1024, width))
                total = total + nn(hz[h, i], mzbuf[:, :, :, :, :, cols].reshape(1024, width))
                zd[h, i, :, pl.ds(at, width)] = total.astype(bf16)
        cp = remote(zd.at[h, 1], d_a.at[:, pl.ds(h * F, F)], ds.at[h], dr.at[h], dev(dz=step[1 - h]))
        cp.start()
        sent3.append(cp)
        cp = pltpu.make_async_copy(zd.at[h, 0], d_own.at[:, pl.ds(h * F, F)], zl.at[6 + h])
        cp.start()
        units["d", h] = cp

    def hidden_grad(j, n):
        def one(k, _):
            a, b = k // 2, k % 2
            grad = nt(mgbuf[a, b].reshape(256, D), wd[pl.ds(j * T, n * T), :])
            for i in range(n):
                part_grad = grad[:, i * T : (i + 1) * T]
                for m in range(2):
                    cols = pl.ds(((j + i) * 2 + m) * T, T)
                    au[a, b, :, cols] = (part_grad * au[a, b, :, cols].astype(f32)).astype(bf16)
            return 0

        lax.fori_loop(0, 4, one, 0)

    def in_grads(j):
        def one(i, _):
            to = (z + 2 + i) % 4
            rhs = au[:, :, :, pl.ds(j * 2 * T, 2 * T)].reshape(1024, 2 * T)
            lhs = ntr[pl.ds(pl.multiple_of(to * 288, 32), 288), :]
            total = nn(lhs, rhs).astype(bf16)
            zg[j, to] = total[:, :T]
            zu[j, to] = total[:, T:]
            return 0

        lax.fori_loop(0, 1, one, 0)
        z_first("g", j)
        z_first("u", j)
        lax.fori_loop(1, 4, one, 0)
        z_own("g", j)
        z_own("u", j)

    for h in range(2):
        ref = mzbuf.at[yl, yh, x, c].at[mz_half(h)]
        remote(ref, ref, ms.at[h], mr.at[h], dev(dz=step[h])).wait_recv()
    steps = gather(mzbuf, ag3s, ag3r, sent2)
    next(steps)
    hidden_grad(0, 1)
    in_grads(0)
    next(steps)
    hidden_grad(1, 2)
    next(steps)
    in_grads(1)
    z_second("g", 0)
    z_second("u", 0)
    next(steps)
    in_grads(2)
    next(steps)
    z_second("g", 1)
    z_second("u", 1)

    def normed_grad(half):
        def one(j, _):
            total = nt(au[yl, half], wgu[tile(j, 2 * T), :])
            part[half, :, :, :, tile(j, 2 * T)] = total.astype(bf16).reshape(4, 2, B, 2 * T)
            return 0

        lax.fori_loop(0, 3, one, 0)

    normed_grad(1 - yh)
    pend = [core_send(1 - yh, 0, rs2s, rs2r)]
    next(steps)
    next(steps)
    z_second("g", 2)
    z_second("u", 2)
    sum_first(rs2s, rs2r)
    normed_grad(yh)
    pend.append(core_send(yh, 1, rs2s, rs2r))
    next(steps)
    sum_second(rs2s, rs2r)
    run(steps)
    down_grad(0)
    sum_third(rs2s, rs2r)
    down_grad(1)
    grad_in = sum_last(rs2s, rs2r)
    tok_f = tok[...].astype(f32)
    recip_in = lax.rsqrt(jnp.mean(tok_f * tok_f, axis=-1, keepdims=True) + epsilon)
    scaled_in = tok_f * recip_in
    weighted = grad_in * gpre
    back = recip_in * (weighted - scaled_in * jnp.mean(weighted * scaled_in, axis=-1, keepdims=True))
    tgrad[...] = (cot[...].astype(f32) + back).astype(bf16)
    g_x[x * 2 + c, 0:1, :] = jnp.sum(grad_in * scaled_in, axis=0, keepdims=True)

    def exchange(slots, me, peers, base, place):
        cps = []
        for n, o in enumerate(peers):
            cp = remote(slots.at[me], slots.at[me], gs.at[base + n], gr.at[base + n], dev(**o))
            cp.start()
            cps.append(cp)
        for n, o in enumerate(peers):
            ref = slots.at[place({k: -v for k, v in o.items()})]
            remote(ref, ref, gs.at[base + n], gr.at[base + n], dev(**o)).wait_recv()
        value = slots[0]
        for n in range(1, len(peers) + 1):
            value = value + slots[n]
        return value, cps

    value, cps = exchange(
        g_x, x * 2 + c, chips_x, 0, lambda o: ((x + o["dx"] + 4) % 4) * 2 + (c + o["dc"] + 2) % 2
    )
    sent3 += cps
    g_yz[y * 4 + z] = value
    value, cps = exchange(
        g_yz, y * 4 + z, chips_yz, 7, lambda o: ((y + o["dy"] + 4) % 4) * 4 + (z + o["dz"] + 4) % 4
    )
    sent3 += cps
    gain_out[...] = value

    for kind in "gu":
        _, _, own, out_a, out_b, base = bufs[kind]
        for j in range(3):
            q = (base + j) * 4
            for k, out in ((0, out_a), (1, out_b)):
                ref = out.at[:, pl.ds(j * T, T)]
                remote(ref, ref, zs.at[q + 2 + k], zr.at[q + 2 + k], dev(dz=1)).wait_recv()
            units[kind, j].wait()
    for h in range(2):
        ref = d_a.at[:, pl.ds(h * F, F)]
        remote(ref, ref, ds.at[h], dr.at[h], dev(dz=1)).wait_recv()
        units["d", h].wait()
    for cp in pend + sent2 + sent3:
        cp.wait_send()
    sum_wait(rs2s, rs2r)


def finish(
    bout, tgrad, gains, d_own, d_a, g_own, g_a, g_b, u_own, u_a, u_b,
    bout_out, tgrad_out, pre_out, post_out, gate_out, up_out, down_out,
):
    bout_out[...] = bout[...]
    tgrad_out[...] = tgrad[...]
    pre_out[...] = gains[0, :]
    post_out[...] = gains[1, :]
    gate_out[...] = (g_own[...].astype(f32) + g_a[...].astype(f32)) + g_b[...].astype(f32)
    up_out[...] = (u_own[...].astype(f32) + u_a[...].astype(f32)) + u_b[...].astype(f32)
    down_out[...] = d_own[...].astype(f32) + d_a[...].astype(f32)


def local(tokens, gain_pre, gain_post, gate_weight, up_weight, down_weight, cotangent):
    vm = pl.BlockSpec(memory_space=pltpu.VMEM)
    hbm = pl.BlockSpec(memory_space=pl.ANY)
    S = jax.ShapeDtypeStruct
    dma = pltpu.SemaphoreType.DMA
    V = pltpu.VMEM
    outs = pl.pallas_call(
        kernel,
        out_shape=(
            [S((B, D), bf16), S((B, D), bf16), S((2, D), f32)]
            + [S((144, D), bf16)] * 2
            + [S((288, F), bf16)] * 6
        ),
        in_specs=[vm] * 4 + [hbm] * 3,
        out_specs=[vm] * 3 + [hbm] * 8,
        scratch_shapes=[
            V((D, 2 * F), bf16),
            V((F, D), bf16),
            V((2, 2, 4, 2, B, D), bf16),
            V((2, 2, 4, 2, B, D), bf16),
            V((2, 2, 4, 2, B, D), bf16),
            V((2, 2, 256, 2 * F), bf16),
            V((2, 256, F), bf16),
            V((F, 1024), bf16),
            V((2, 2, 144, 1024), bf16),
            V((F, 1024), bf16),
            V((2, 4, 2, B, D), bf16),
            V((2, 4, B, D), bf16),
            V((2, 3, B, D), bf16),
            V((B, D), bf16),
            V((B, D), bf16),
            V((4, B, D), bf16),
            V((2, 2, 144, F), bf16),
            V((3, 4, 288, T), bf16),
            V((3, 4, 288, T), bf16),
            V((3, 2, 144, T), bf16),
            V((3, 2, 144, T), bf16),
            V((256, 2 * T), f32),
            V((256, 2 * T), f32),
            V((8, 2, D), f32),
            V((16, 2, D), f32),
            dma((7,)),
            dma((33,)), dma((33,)), dma((32,)), dma((32,)), dma((32,)), dma((32,)),
            dma((9,)), dma((9,)), dma((9,)), dma((9,)),
            dma((24,)), dma((24,)), dma((8,)),
            dma((4,)), dma((4,)), dma((2,)), dma((2,)), dma((2,)), dma((2,)),
            dma((22,)), dma((22,)),
        ],
        compiler_params=pltpu.CompilerParams(
            collective_id=0, has_side_effects=True, vmem_limit_bytes=63 * 2**20
        ),
        cost_estimate=pl.CostEstimate(flops=33 * 10**9, bytes_accessed=30 * 10**6, transcendentals=0),
    )(
        tokens, cotangent, gain_pre, gain_post,
        gate_weight, up_weight, down_weight,
    )

    def whole(*shape):
        return pl.BlockSpec(shape, lambda i: (0,) * len(shape))

    def rows(n, width):
        return pl.BlockSpec((n, width), lambda i: (i, 0))

    n = 1
    return pl.pallas_call(
        finish,
        grid=(n,),
        out_shape=[
            S((B, D), bf16), S((B, D), bf16), S((D,), f32), S((D,), f32),
            S((288, F), f32), S((288, F), f32), S((144, D), f32),
        ],
        in_specs=[whole(B, D), whole(B, D), whole(2, D)] + [rows(144 // n, D)] * 2 + [rows(288 // n, F)] * 6,
        out_specs=[whole(B, D), whole(B, D), whole(D), whole(D)]
        + [rows(288 // n, F)] * 2 + [rows(144 // n, D)],
    )(*outs)


def solution(mesh):
    in_specs = (
        P(("dp", "tp"), None),
        P(),
        P(),
        P(None, "tp"),
        P(None, "tp"),
        P("tp", None),
        P(("dp", "tp"), None),
    )
    out_specs = (
        P(("dp", "tp"), None),
        P(("dp", "tp"), None),
        P(),
        P(),
        P("dp", "tp"),
        P("dp", "tp"),
        P(("tp", "dp"), None),
    )
    return jax.shard_map(local, mesh=mesh, in_specs=in_specs, out_specs=out_specs, check_vma=False)
```

```python
import jax
import jax.numpy as jnp
from jax import lax
from jax.experimental import pallas as pl
from jax.experimental.pallas import tpu as pltpu
from jax.sharding import PartitionSpec as P

epsilon = 1e-06
root_two_pi = 0.7978845608028654
MESH = pl.DeviceIdType.MESH
D = 2304
F = 1152
B = 32
T = 384
f32 = jnp.float32
bf16 = jnp.bfloat16


def gelu_pair(values):
    tanh_arg = root_two_pi * (values + 0.044715 * values * values * values)
    hyper = jnp.tanh(tanh_arg)
    gelu_value = 0.5 * values * (1.0 + hyper)
    gelu_slope = 0.5 * (1.0 + hyper) + 0.5 * values * (1.0 - hyper * hyper) * root_two_pi * (
        1.0 + 3.0 * 0.044715 * values * values
    )
    return (gelu_value, gelu_slope)


def nt(a, b):
    return lax.dot_general(a, b, (((1,), (1,)), ((), ())), preferred_element_type=f32)


def nn(a, b):
    return jnp.dot(a, b, preferred_element_type=f32)


def tile(j, width=T):
    return pl.ds(pl.multiple_of(j * width, 128), width)


def kernel(
    tok, cot, gpre_in, gpost_in, wg_h, wu_h, wd_h,
    bout, tgrad, gain_out, d_own, d_a, g_own, g_a, g_b, u_own, u_a, u_b,
    wgu, wd, nbuf, mgbuf, mzbuf, au, hown, ht, hz, ntr, part, crecv, xrecv, ysend, yrecv, yall,
    zd, zg, zu, zgf, zuf, gu0, gu1, g_x, g_yz,
    wsem, ag1s, ag1r, ag2s, ag2r, ag3s, ag3r, rs1s, rs1r, rs2s, rs2r, zs, zr, zl, hs, hr, ms, mr, ds, dr, gs, gr,
):
    dp, tp = lax.axis_index("dp"), lax.axis_index("tp")
    c = tp % 2
    x = (tp // 2) % 4
    yh = tp // 8
    yl = dp // 4
    z = dp % 4
    y = yh * 2 + yl

    def dev(dx=0, dy=0, dz=0, dc=0):
        yy = (y + dy) % 4
        return ((yy % 2) * 4 + (z + dz) % 4, ((yy // 2) * 4 + (x + dx) % 4) * 2 + (c + dc) % 2)

    gate_up = (gu0, gu1)
    gpre = gpre_in[...].reshape(1, D)
    gpost = gpost_in[...].reshape(1, D)

    loads = [
        pltpu.make_async_copy(
            h.at[:, pl.ds(j * T, T)], wgu.at[:, pl.ds((2 * j + k) * T, T)], wsem.at[2 * j + k]
        )
        for j in range(3)
        for k, h in enumerate((wg_h, wu_h))
    ] + [pltpu.make_async_copy(wd_h, wd, wsem.at[6])]

    barrier = pltpu.get_barrier_semaphore()
    chips_x = [dict(dx=i, dc=j) for i in range(4) for j in range(2) if i + j]
    chips_yz = [dict(dy=i, dz=j) for i in range(4) for j in range(4) if i + j]
    offs = chips_x + chips_yz
    for o in offs:
        pl.semaphore_signal(barrier, inc=1, device_id=dev(**o), device_id_type=MESH)

    def remote(src, dst, s, r, to):
        return pltpu.make_async_remote_copy(
            src_ref=src, dst_ref=dst, send_sem=s, recv_sem=r, device_id=to, device_id_type=MESH
        )

    def blk(buf, df, ds, core=None):
        dx = df * (1 - c) + ds * c
        dy = df * c + ds * (1 - c)
        xx, yy = (x + dx) % 4, (y + dy) % 4
        return buf.at[yy % 2, yy // 2, xx, c]

    def other_blk(buf, df, ds):
        dx = df * c + ds * (1 - c)
        dy = df * (1 - c) + ds * c
        xx, yy = (x + dx) % 4, (y + dy) % 4
        return buf.at[yy % 2, yy // 2, xx, 1 - c]

    def to_f(sign):
        return dev(dx=(1 - c) * (sign % 4), dy=c * (sign % 4))

    def to_s(sign):
        return dev(dx=c * (sign % 4), dy=(1 - c) * (sign % 4))

    def gather(buf, ss, rr, sent):
        def send(i, ref, to):
            cp = remote(ref, ref, ss.at[i], rr.at[i], to)
            cp.start()
            sent.append(cp)

        def got(i, ref):
            remote(ref, ref, ss.at[i], rr.at[i], dev(dc=1)).wait_recv()

        def core(df, ds):
            send(16 + ds * 4 + df, blk(buf, df, ds), dev(dc=1))

        own = blk(buf, 0, 0)
        send(0, own, to_f(1))
        send(1, own, to_f(-1))
        send(4, own, to_s(1))
        send(8, own, to_s(-1))
        core(0, 0)
        yield
        got(0, blk(buf, 3, 0))
        send(2, blk(buf, 3, 0).at[pl.ds(0, 16)], to_f(1))
        send(7, blk(buf, 3, 0), to_s(1))
        send(11, blk(buf, 3, 0), to_s(-1))
        core(3, 0)
        got(1, blk(buf, 1, 0))
        send(3, blk(buf, 1, 0).at[pl.ds(16, 16)], to_f(-1))
        send(5, blk(buf, 1, 0), to_s(1))
        send(9, blk(buf, 1, 0), to_s(-1))
        core(1, 0)
        yield
        got(2, blk(buf, 2, 0).at[pl.ds(0, 16)])
        got(3, blk(buf, 2, 0).at[pl.ds(16, 16)])
        send(6, blk(buf, 2, 0), to_s(1))
        send(10, blk(buf, 2, 0), to_s(-1))
        core(2, 0)
        yield
        for df, fwd_a, fwd_b in ((0, 12, None), (1, 13, None), (3, None, 14), (2, None, 15)):
            got(4 + df, blk(buf, df, 3))
            if fwd_a is not None:
                send(fwd_a, blk(buf, df, 3), to_s(1))
            core(df, 3)
            got(8 + df, blk(buf, df, 1))
            if fwd_b is not None:
                send(fwd_b, blk(buf, df, 1), to_s(-1))
            core(df, 1)
            yield
        for i, df in ((12, 0), (13, 1), (14, 3), (15, 2)):
            got(i, blk(buf, df, 2))
            core(df, 2)
        yield
        for ds in range(4):
            for df in range(4):
                got(16 + ds * 4 + df, other_blk(buf, df, ds))

    def group_gather(buf, ss, rr, sent):
        def at(dx, dy, core=c):
            yy = (y + dy) % 4
            return buf.at[yy % 2, yy // 2, (x + dx) % 4, core]

        def send(i, ref, **to):
            cp = remote(ref, ref, ss.at[i], rr.at[i], dev(**to))
            cp.start()
            sent.append(cp)

        def got(i, ref):
            remote(ref, ref, ss.at[i], rr.at[i], dev(dc=1)).wait_recv()

        low, high = pl.ds(0, 16), pl.ds(16, 16)
        own = at(0, 0)
        send(0, own, dy=2)
        send(1, own, dx=1)
        send(2, own, dx=3)
        send(5, own, dc=1)
        yield
        got(0, at(0, 2))
        send(6, at(0, 2), dx=1)
        send(7, at(0, 2), dx=3)
        send(8, at(0, 2), dc=1)
        send(3, own, dy=1)
        send(4, own, dy=3)
        yield
        got(1, at(3, 0))
        send(9, at(3, 0).at[low], dx=1)
        send(12, at(3, 0), dc=1)
        got(2, at(1, 0))
        send(13, at(1, 0).at[high], dx=3)
        send(16, at(1, 0), dc=1)
        for i, dx in ((10, 3), (14, 1)):
            send(i, at(dx, 0), dy=1)
            send(i + 1, at(dx, 0), dy=3)
        yield
        got(6, at(3, 2))
        send(20, at(3, 2).at[low], dx=1)
        send(21, at(3, 2), dc=1)
        got(7, at(1, 2))
        send(22, at(1, 2).at[high], dx=3)
        send(23, at(1, 2), dc=1)
        got(9, at(2, 0).at[low])
        got(13, at(2, 0).at[high])
        send(19, at(2, 0), dc=1)
        send(17, at(2, 0), dy=1)
        send(18, at(2, 0), dy=3)
        got(20, at(2, 2).at[low])
        got(22, at(2, 2).at[high])
        send(24, at(2, 2), dc=1)
        for i, dx, dy in ((5, 0, 0), (8, 0, 2), (12, 3, 0), (16, 1, 0), (21, 3, 2), (23, 1, 2), (19, 2, 0), (24, 2, 2)):
            got(i, at(dx, dy, 1 - c))
        yield
        rest = [(i + k, dx, 3 - 2 * k) for i, dx in ((3, 0), (10, 3), (14, 1), (17, 2)) for k in (0, 1)]
        for n, (i, dx, dy) in enumerate(rest):
            got(i, at(dx, dy))
            send(25 + n, at(dx, dy), dc=1)
        yield
        for n, (i, dx, dy) in enumerate(rest):
            got(25 + n, at(dx, dy, 1 - c))

    def run(steps):
        for _ in steps:
            pass

    def core_send(half, i, ss, rr):
        cp = remote(part.at[half, :, 1 - c], crecv.at[i], ss.at[i], rr.at[i], dev(dc=1))
        cp.start()
        return cp

    def core_add(half, i, ss, rr):
        remote(crecv.at[i], crecv.at[i], ss.at[i], rr.at[i], dev(dc=1)).wait_recv()

        def one(k, _):
            part[half, k, c] = (part[half, k, c].astype(f32) + crecv[i, k].astype(f32)).astype(bf16)
            return 0

        lax.fori_loop(0, 4, one, 0)

    def x_copies(half, i, ss, rr):
        out = []
        for dx in (2, 1, 3):
            k = 2 + i * 3 + dx - 1
            out.append(remote(
                part.at[half, (x + dx) % 4, c], xrecv.at[i, dx - 1], ss.at[k], rr.at[k], dev(dx=dx)
            ))
        return out

    def x_sum(half, i, ss, rr):
        for dx in (1, 3, 2):
            k = 2 + i * 3 + dx - 1
            ref = xrecv.at[i, dx - 1]
            remote(ref, ref, ss.at[k], rr.at[k], dev(dx=dx)).wait_recv()
        total = part[half, x, c].astype(f32)
        for dx in (1, 3, 2):
            total = total + xrecv[i, dx - 1].astype(f32)
        return total

    def y_copy(ss, rr):
        return remote(ysend, yrecv, ss.at[8], rr.at[8], dev(dy=2))

    def y_copy_all(ss, rr):
        return remote(part.at[1 - yh, :, c], yall, ss.at[8], rr.at[8], dev(dy=2))

    def start(copies):
        for cp in copies:
            cp.start()

    def sum_first(ss, rr):
        core_add(1 - yh, 0, ss, rr)

        @pl.when(c == 0)
        def _():
            start(x_copies(1 - yh, 0, ss, rr))

        @pl.when(c == 1)
        def _():
            start([y_copy_all(ss, rr)])

    def sum_second(ss, rr):
        core_add(yh, 1, ss, rr)

        @pl.when(c == 0)
        def _():
            start(x_copies(yh, 1, ss, rr))

    def sum_third(ss, rr):
        @pl.when(c == 0)
        def _():
            ysend[...] = x_sum(1 - yh, 0, ss, rr).astype(bf16)
            start([y_copy(ss, rr)])

        @pl.when(c == 1)
        def _():
            y_copy_all(ss, rr).wait_recv()

            def one(k, _):
                part[yh, k, c] = (part[yh, k, c].astype(f32) + yall[k].astype(f32)).astype(bf16)
                return 0

            lax.fori_loop(0, 4, one, 0)
            start(x_copies(yh, 1, ss, rr))

    def sum_last(ss, rr):
        total = x_sum(yh, 1, ss, rr)

        @pl.when(c == 0)
        def _():
            y_copy(ss, rr).wait_recv()

        return total + yrecv[...].astype(f32)

    def sum_wait(ss, rr):
        @pl.when(c == 0)
        def _():
            for cp in x_copies(1 - yh, 0, ss, rr) + [y_copy(ss, rr)]:
                cp.wait_send()

        @pl.when(c == 1)
        def _():
            y_copy_all(ss, rr).wait_send()

        for cp in x_copies(yh, 1, ss, rr):
            cp.wait_send()

    @pl.when(c == 1)
    def _():
        yrecv[...] = jnp.zeros_like(yrecv)

    tok_f = tok[...].astype(f32)
    recip_in = lax.rsqrt(jnp.mean(tok_f * tok_f, axis=-1, keepdims=True) + epsilon)
    nbuf[yl, yh, x, c] = (tok_f * recip_in * gpre).astype(bf16)

    pl.semaphore_wait(barrier, len(offs))
    sent1 = []
    steps = group_gather(nbuf, ag1s, ag1r, sent1)
    for some in (loads[0:2], loads[2:4], loads[4:7]):
        next(steps)
        for load in some:
            load.start()
    next(steps)
    for load in loads:
        load.wait()

    def forward(a, b, is_own, between=None):
        rows = nbuf[a, b].reshape(256, D)
        for j in range(4):
            if j < 3:
                gate_up[j % 2][...] = nn(rows, wgu[:, pl.ds(j * 2 * T, 2 * T)])
            if j > 0:
                cols = pl.ds((j - 1) * T, T)
                up = gate_up[(j - 1) % 2][:, T:]
                value, slope = gelu_pair(gate_up[(j - 1) % 2][:, :T])
                hidden = (value * up).astype(bf16)
                au[a, b, :, pl.ds((j - 1) * 2 * T, T)] = (up * slope).astype(bf16)
                au[a, b, :, pl.ds((j - 1) * 2 * T + T, T)] = value.astype(bf16)
                if is_own:
                    hown[b, :, cols] = hidden
                ht[cols, tile(a * 2 + b, 256)] = hidden.T
            if between is not None and j == 1:
                between()

    def down(half):
        def one(j, _):
            part[half, :, :, :, tile(j, 2 * T)] = (
                nn(hown[half], wd[:, tile(j, 2 * T)]).astype(bf16).reshape(4, 2, B, 2 * T)
            )
            return 0

        lax.fori_loop(0, 3, one, 0)

    forward(yl, 1 - yh, True)
    down(1 - yh)
    pend = [core_send(1 - yh, 0, rs1s, rs1r)]

    forward(yl, yh, True, lambda: sum_first(rs1s, rs1r))
    down(yh)
    pend.append(core_send(yh, 1, rs1s, rs1r))
    next(steps)
    sum_second(rs1s, rs1r)
    run(steps)
    forward(1 - yl, 0, False)
    sum_third(rs1s, rs1r)
    forward(1 - yl, 1, False)

    sent2 = []
    near = (z + 1 - 2 * (z % 2), 3 - z)
    step = (1 + 2 * (z % 2), 3 - 2 * (z % 2))

    def shards(q):
        flip = q + 1 - 2 * (q % 2)
        return ((q, 3 - q), (q, flip))

    def ht_rows(q):
        return pl.ds(pl.multiple_of((yl * 4 + q) * 144, 16), 144)

    for h in range(2):
        for i in range(2):
            cp = remote(ht.at[ht_rows(shards(near[h])[h][i])], hz.at[h, i], hs.at[h * 2 + i], hr.at[h * 2 + i], dev(dz=step[h]))
            cp.start()
            sent2.append(cp)

    mixed = sum_last(rs1s, rs1r)

    recip_mix = lax.rsqrt(jnp.mean(mixed * mixed, axis=-1, keepdims=True) + epsilon)
    scaled_mix = mixed * recip_mix
    cot_f = cot[...].astype(f32)
    weighted = cot_f * gpost
    mix_grad = recip_mix * (
        weighted - scaled_mix * jnp.mean(weighted * scaled_mix, axis=-1, keepdims=True)
    )
    mgbuf[yl, yh, x, c] = mix_grad.astype(bf16)
    for cp in pend + sent1:
        cp.wait_send()
    sum_wait(rs1s, rs1r)

    def mz_half(h):
        return (pl.ds(0, B), pl.ds(h * F, F))

    for h in range(2):
        cp = remote(
            mgbuf.at[yl, yh, x, c].at[mz_half(h)], mzbuf.at[yl, yh, x, c].at[mz_half(h)], ms.at[h], mr.at[h], dev(dz=step[h])
        )
        cp.start()
        sent2.append(cp)
    steps = gather(mgbuf, ag2s, ag2r, sent2)
    next(steps)
    bout[...] = (tok[...].astype(f32) + scaled_mix * gpost).astype(bf16)
    g_x[x * 2 + c, 1:2, :] = jnp.sum(cot_f * scaled_mix, axis=0, keepdims=True)
    next(steps)
    next(steps)

    def turn(k, _):
        def one(j, _):
            cols = pl.ds(pl.multiple_of(yl * F + j * T, 128), T)
            ntr[tile(j), tile(k, 256)] = nbuf[k // 2, k % 2, :, :, :, cols].reshape(256, T).T
            return 0

        lax.fori_loop(0, 3, one, 0)
        return 0

    lax.fori_loop(0, 2, turn, 0)
    next(steps)
    lax.fori_loop(2, 4, turn, 0)
    run(steps)

    units = {}
    sent3 = []

    bufs = {"g": (zg, zgf, g_own, g_a, g_b, 0), "u": (zu, zuf, u_own, u_a, u_b, 3)}

    def z_first(kind, j):
        buf, fwd, own, _, _, base = bufs[kind]
        q = (base + j) * 4
        for k, dz in ((0, 1), (1, 3)):
            cp = remote(
                buf.at[j, (z + 2) % 4].at[pl.ds(k * 144, 144)], fwd.at[j, k], zs.at[q + k], zr.at[q + k], dev(dz=dz)
            )
            cp.start()
            sent3.append(cp)

    def z_own(kind, j):
        buf, _, own, _, _, base = bufs[kind]
        cp = pltpu.make_async_copy(buf.at[j, z], own.at[:, pl.ds(j * T, T)], zl.at[base + j])
        cp.start()
        units[kind, j] = cp

    def z_second(kind, j):
        buf, fwd, _, out_a, out_b, base = bufs[kind]
        q = (base + j) * 4
        for k, dz, out in ((0, 1, out_a), (1, 3, out_b)):
            ref = fwd.at[j, k]
            remote(ref, ref, zs.at[q + k], zr.at[q + k], dev(dz=dz)).wait_recv()
            to = (z + dz) % 4
            rows = pl.ds(k * 144, 144)
            buf[j, to, rows] = (buf[j, to, rows].astype(f32) + fwd[j, k].astype(f32)).astype(bf16)
            cp = remote(
                buf.at[j, to], out.at[:, pl.ds(j * T, T)], zs.at[q + 2 + k], zr.at[q + 2 + k], dev(dz=dz)
            )
            cp.start()
            sent3.append(cp)

    def down_grad(h):
        for i in range(2):
            ref = hz.at[h, i]
            remote(ref, ref, hs.at[h * 2 + i], hr.at[h * 2 + i], dev(dz=step[h])).wait_recv()
        mine = shards(z)[h]
        for i in range(2):
            for at, width in ((0, 2 * T), (2 * T, T)):
                cols = pl.ds(h * F + at, width)
                total = nn(ht[ht_rows(mine[i]), :], mgbuf[:, :, :, :, :, cols].reshape(1024, width))
                total = total + nn(hz[h, i], mzbuf[:, :, :, :, :, cols].reshape(1024, width))
                zd[h, i, :, pl.ds(at, width)] = total.astype(bf16)
        cp = remote(zd.at[h, 1], d_a.at[:, pl.ds(h * F, F)], ds.at[h], dr.at[h], dev(dz=step[1 - h]))
        cp.start()
        sent3.append(cp)
        cp = pltpu.make_async_copy(zd.at[h, 0], d_own.at[:, pl.ds(h * F, F)], zl.at[6 + h])
        cp.start()
        units["d", h] = cp

    def hidden_grad(j, n):
        def one(k, _):
            a, b = k // 2, k % 2
            grad = nt(mgbuf[a, b].reshape(256, D), wd[pl.ds(j * T, n * T), :])
            for i in range(n):
                part_grad = grad[:, i * T : (i + 1) * T]
                for m in range(2):
                    cols = pl.ds(((j + i) * 2 + m) * T, T)
                    au[a, b, :, cols] = (part_grad * au[a, b, :, cols].astype(f32)).astype(bf16)
            return 0

        lax.fori_loop(0, 4, one, 0)

    def in_grads(j):
        def one(i, _):
            to = (z + 2 + i) % 4
            rhs = au[:, :, :, pl.ds(j * 2 * T, 2 * T)].reshape(1024, 2 * T)
            lhs = ntr[pl.ds(pl.multiple_of(to * 288, 32), 288), :]
            total = nn(lhs, rhs).astype(bf16)
            zg[j, to] = total[:, :T]
            zu[j, to] = total[:, T:]
            return 0

        lax.fori_loop(0, 1, one, 0)
        z_first("g", j)
        z_first("u", j)
        lax.fori_loop(1, 4, one, 0)
        z_own("g", j)
        z_own("u", j)

    for h in range(2):
        ref = mzbuf.at[yl, yh, x, c].at[mz_half(h)]
        remote(ref, ref, ms.at[h], mr.at[h], dev(dz=step[h])).wait_recv()
    steps = gather(mzbuf, ag3s, ag3r, sent2)
    next(steps)
    hidden_grad(0, 1)
    in_grads(0)
    next(steps)
    hidden_grad(1, 2)
    next(steps)
    in_grads(1)
    z_second("g", 0)
    z_second("u", 0)
    next(steps)
    in_grads(2)
    next(steps)
    z_second("g", 1)
    z_second("u", 1)

    def normed_grad(half):
        def one(j, _):
            total = nt(au[yl, half], wgu[tile(j, 2 * T), :])
            part[half, :, :, :, tile(j, 2 * T)] = total.astype(bf16).reshape(4, 2, B, 2 * T)
            return 0

        lax.fori_loop(0, 3, one, 0)

    normed_grad(1 - yh)
    pend = [core_send(1 - yh, 0, rs2s, rs2r)]
    next(steps)
    next(steps)
    z_second("g", 2)
    z_second("u", 2)
    sum_first(rs2s, rs2r)
    normed_grad(yh)
    pend.append(core_send(yh, 1, rs2s, rs2r))
    next(steps)
    sum_second(rs2s, rs2r)
    run(steps)
    down_grad(0)
    sum_third(rs2s, rs2r)
    down_grad(1)
    grad_in = sum_last(rs2s, rs2r)
    tok_f = tok[...].astype(f32)
    recip_in = lax.rsqrt(jnp.mean(tok_f * tok_f, axis=-1, keepdims=True) + epsilon)
    scaled_in = tok_f * recip_in
    weighted = grad_in * gpre
    back = recip_in * (weighted - scaled_in * jnp.mean(weighted * scaled_in, axis=-1, keepdims=True))
    tgrad[...] = (cot[...].astype(f32) + back).astype(bf16)
    g_x[x * 2 + c, 0:1, :] = jnp.sum(grad_in * scaled_in, axis=0, keepdims=True)

    def exchange(slots, me, peers, base, place):
        cps = []
        for n, o in enumerate(peers):
            cp = remote(slots.at[me], slots.at[me], gs.at[base + n], gr.at[base + n], dev(**o))
            cp.start()
            cps.append(cp)
        for n, o in enumerate(peers):
            ref = slots.at[place({k: -v for k, v in o.items()})]
            remote(ref, ref, gs.at[base + n], gr.at[base + n], dev(**o)).wait_recv()
        value = slots[0]
        for n in range(1, len(peers) + 1):
            value = value + slots[n]
        return value, cps

    value, cps = exchange(
        g_x, x * 2 + c, chips_x, 0, lambda o: ((x + o["dx"] + 4) % 4) * 2 + (c + o["dc"] + 2) % 2
    )
    sent3 += cps
    g_yz[y * 4 + z] = value
    value, cps = exchange(
        g_yz, y * 4 + z, chips_yz, 7, lambda o: ((y + o["dy"] + 4) % 4) * 4 + (z + o["dz"] + 4) % 4
    )
    sent3 += cps
    gain_out[...] = value

    for kind in "gu":
        _, _, own, out_a, out_b, base = bufs[kind]
        for j in range(3):
            q = (base + j) * 4
            for k, out in ((0, out_a), (1, out_b)):
                ref = out.at[:, pl.ds(j * T, T)]
                remote(ref, ref, zs.at[q + 2 + k], zr.at[q + 2 + k], dev(dz=1)).wait_recv()
            units[kind, j].wait()
    for h in range(2):
        ref = d_a.at[:, pl.ds(h * F, F)]
        remote(ref, ref, ds.at[h], dr.at[h], dev(dz=1)).wait_recv()
        units["d", h].wait()
    for cp in pend + sent2 + sent3:
        cp.wait_send()
    sum_wait(rs2s, rs2r)


def finish(
    bout, tgrad, gains, d_own, d_a, g_own, g_a, g_b, u_own, u_a, u_b,
    bout_out, tgrad_out, pre_out, post_out, gate_out, up_out, down_out,
):
    bout_out[...] = bout[...]
    tgrad_out[...] = tgrad[...]
    pre_out[...] = gains[0, :]
    post_out[...] = gains[1, :]
    gate_out[...] = (g_own[...].astype(f32) + g_a[...].astype(f32)) + g_b[...].astype(f32)
    up_out[...] = (u_own[...].astype(f32) + u_a[...].astype(f32)) + u_b[...].astype(f32)
    down_out[...] = d_own[...].astype(f32) + d_a[...].astype(f32)


def local(tokens, gain_pre, gain_post, gate_weight, up_weight, down_weight, cotangent):
    vm = pl.BlockSpec(memory_space=pltpu.VMEM)
    hbm = pl.BlockSpec(memory_space=pl.ANY)
    S = jax.ShapeDtypeStruct
    dma = pltpu.SemaphoreType.DMA
    V = pltpu.VMEM
    outs = pl.pallas_call(
        kernel,
        out_shape=(
            [S((B, D), bf16), S((B, D), bf16), S((2, D), f32)]
            + [S((144, D), bf16)] * 2
            + [S((288, F), bf16)] * 6
        ),
        in_specs=[vm] * 4 + [hbm] * 3,
        out_specs=[vm] * 3 + [hbm] * 8,
        scratch_shapes=[
            V((D, 2 * F), bf16),
            V((F, D), bf16),
            V((2, 2, 4, 2, B, D), bf16),
            V((2, 2, 4, 2, B, D), bf16),
            V((2, 2, 4, 2, B, D), bf16),
            V((2, 2, 256, 2 * F), bf16),
            V((2, 256, F), bf16),
            V((F, 1024), bf16),
            V((2, 2, 144, 1024), bf16),
            V((F, 1024), bf16),
            V((2, 4, 2, B, D), bf16),
            V((2, 4, B, D), bf16),
            V((2, 3, B, D), bf16),
            V((B, D), bf16),
            V((B, D), bf16),
            V((4, B, D), bf16),
            V((2, 2, 144, F), bf16),
            V((3, 4, 288, T), bf16),
            V((3, 4, 288, T), bf16),
            V((3, 2, 144, T), bf16),
            V((3, 2, 144, T), bf16),
            V((256, 2 * T), f32),
            V((256, 2 * T), f32),
            V((8, 2, D), f32),
            V((16, 2, D), f32),
            dma((7,)),
            dma((33,)), dma((33,)), dma((32,)), dma((32,)), dma((32,)), dma((32,)),
            dma((9,)), dma((9,)), dma((9,)), dma((9,)),
            dma((24,)), dma((24,)), dma((8,)),
            dma((4,)), dma((4,)), dma((2,)), dma((2,)), dma((2,)), dma((2,)),
            dma((22,)), dma((22,)),
        ],
        compiler_params=pltpu.CompilerParams(
            collective_id=0, has_side_effects=True, vmem_limit_bytes=63 * 2**20
        ),
        cost_estimate=pl.CostEstimate(flops=33 * 10**9, bytes_accessed=30 * 10**6, transcendentals=0),
    )(
        tokens, cotangent, gain_pre, gain_post,
        gate_weight, up_weight, down_weight,
    )

    def whole(*shape):
        return pl.BlockSpec(shape, lambda i: (0,) * len(shape))

    def rows(n, width):
        return pl.BlockSpec((n, width), lambda i: (i, 0))

    n = 1
    return pl.pallas_call(
        finish,
        grid=(n,),
        out_shape=[
            S((B, D), bf16), S((B, D), bf16), S((D,), f32), S((D,), f32),
            S((288, F), f32), S((288, F), f32), S((144, D), f32),
        ],
        in_specs=[whole(B, D), whole(B, D), whole(2, D)] + [rows(144 // n, D)] * 2 + [rows(288 // n, F)] * 6,
        out_specs=[whole(B, D), whole(B, D), whole(D), whole(D)]
        + [rows(288 // n, F)] * 2 + [rows(144 // n, D)],
    )(*outs)


def solution(mesh):
    in_specs = (
        P(("dp", "tp"), None),
        P(),
        P(),
        P(None, "tp"),
        P(None, "tp"),
        P("tp", None),
        P(("dp", "tp"), None),
    )
    out_specs = (
        P(("dp", "tp"), None),
        P(("dp", "tp"), None),
        P(),
        P(),
        P("dp", "tp"),
        P("dp", "tp"),
        P(("tp", "dp"), None),
    )
    return jax.shard_map(local, mesh=mesh, in_specs=in_specs, out_specs=out_specs, check_vma=False)
```
